32 devices in a mesh: pose: 2 (over y), occ: 4 (over z), aux: 2 (over x), rep: 2 (over core).
Axes of the slice: x: 2, y: 2, z: 4, core: 2. Of those that a mesh axis runs over, the one named last changes fastest.
Arguments:
- three_index: bfloat16 [16, 7680, 256], P(('pose', 'occ'), ('aux', 'rep')), parts along dimension 0, may hold values from -0.625 to 0.625
- valid_columns: int32 [16], P(('pose', 'occ')), parts along dimension 0, may hold values from 1 to 256, 1152 in all
- domain_blocks: int32 [16, 2], P(('pose', 'occ')), parts along dimension 0, may hold values from 0 to 63, as said below
- occupied_energy: float32 [16], P(('pose', 'occ')), parts along dimension 0, may hold values from -2 to -0.3
- virtual_energy: float32 [16384], P('pose'), parts along dimension 0, may hold values from 0.2 to 3
- shell_index: int32 [7680], P(('aux', 'rep')), may hold values from 0 to 1535, never falling along the last dimension, each value on 1 to 9 neighbouring positions
- centre_weights: float32 [3, 15360], P(None, ('pose', 'aux', 'rep')), parts along dimension 1, may hold values from -1.5 to 1.5
Outputs:
- gamma_tiles: bfloat16 [16, 7680, 256], P(('pose', 'occ'), ('aux', 'rep')), parts along dimension 0
- shell_gradient: float32 [3, 3072], P(None, ('pose', 'occ', 'aux', 'rep')), parts along dimension 1
The draws below stay inside these ranges and needn't reach their ends.
There are 2 independent parts, one for each index of `pose`. The reference program is written for one: setup_inputs(seed, part) draws one part's arguments, and reference() takes and returns one part's arrays. A program takes and returns all parts, laid end to end along the dimension named above; an argument that names none is the same for every part. Nothing has to cross between parts.
Inputs may be any that keep to these rules, and one draw needn't show every extreme that they name: `domain_blocks`: each row names 2 different tiles; some row names tile 0 and some row tile 64 - 1. `valid_columns`: some orbital has all 256 columns valid. `shell_index`: never falling; every shell holds 1 to 9 consecutive functions, some exactly 9.
All inputs are finite; a program needn't handle non-finite values. No bound on the sum of `valid_columns` on one device may be relied on, other than what follows from the above.
Results may differ from the reference program's by a relative error of at most 0.012.
Values may be sent and summed in bfloat16 or wider, within the bound.
No kernel may reach another device: no remote copies, remote signals or barrier semaphores. Data moves between devices by JAX's collectives and lax.ppermute only.
A program may use at most 64 MiB of HBM per device.

```python
import math
import jax
import jax.numpy as jnp
import numpy as np
from jax import lax

ROWS_DEV = 1920
OCC_DEV = 2
VBW = 128
DOM = 2
VB = 64
NVIR = 8192
NAUX = 7680
NOCC = 8
NSHELL = 1536
N_OCC = 4
N_AUX = 2
N_REP = 2


def draw_domain_blocks(key, part):
    key = jax.random.fold_in(key, 7)
    starting = jax.random.randint(key, (NOCC, 1), 0, VB, dtype=jnp.int32)
    row_number = jnp.arange(NOCC, dtype=jnp.int32)[:, None]
    starting = jnp.where(row_number == 0, VB - 1, starting)
    starting = jnp.where(row_number == 1, 0, starting)
    stride = VB // DOM
    return ((starting + jnp.arange(DOM, dtype=jnp.int32)[None, :] * stride) % VB).astype(jnp.int32)


def levels(stream_key, extent, pieces, smallest, largest):
    loudness, own = 1.0, jax.random.fold_in(stream_key, 6)
    for position, blocks in pieces:
        draws = jnp.exp(jax.random.uniform(jax.random.fold_in(own, position), (blocks,), jnp.float32, smallest / len(pieces), largest / len(pieces)))
        loudness = loudness * jnp.repeat(draws, extent[position] // blocks).reshape([-1 if axis == position else 1 for axis in range(len(extent))])
    return loudness


def split_up(number_of, total, reach, skew):
    loads = [(1 << 20) // math.isqrt(rank ** skew) + 1 for rank in range(2, number_of + 1)]
    surplus, holding = total - reach - (number_of - 1), [1] * (number_of - 1)
    while surplus > 0:
        candidates = [i for i in range(number_of - 1) if holding[i] < reach]
        pool, left = sum([loads[i] for i in candidates]), surplus
        for i in candidates:
            addition = min(reach - holding[i], max(1, left * loads[i] // pool), surplus)
            holding[i] = holding[i] + addition
            surplus = surplus - addition
    return np.array([reach] + holding)


def ragged_sizes(stream_key, number_of, total, reach, slope):
    if number_of == 2:
        one = jax.random.randint(stream_key, (), max(1, total - reach), min(reach, total - 1) + 1)
        return jnp.stack([one, total - one])
    sizes = jnp.asarray(split_up(number_of, total, reach, slope), jnp.int32)
    couples = (number_of - 1) // 2
    source_of, sink = sizes[1:1 + 2 * couples:2], sizes[2:2 + 2 * couples:2]
    slack = jnp.minimum(source_of - 1, reach - sink)
    moved = jax.random.randint(jax.random.fold_in(stream_key, 1), (couples,), 0, 1 << 20) % (slack + 1)
    sizes = sizes.at[1:1 + 2 * couples:2].set(source_of - moved).at[2:2 + 2 * couples:2].set(sink + moved)
    return sizes[jax.random.permutation(jax.random.fold_in(stream_key, 2), number_of)]


def centred(rng, extent, width, limit, cuts=(), kind=jnp.bfloat16):
    drawn = width * jax.random.normal(rng, extent, jnp.float32)
    if cuts:
        drawn = drawn * levels(rng, extent, cuts, -0.22, 0.18)
    return jnp.clip(drawn, -limit, limit).astype(kind)


def setup_inputs(seed: int = 0, part: int = 0) -> dict:
    key_list = jax.random.split(jax.random.key(seed), 8)
    part_splits = jax.random.split(jax.random.fold_in(key_list[7], part), 8)
    return {
        "three_index": centred(part_splits[0], (NOCC, NAUX, DOM * VBW), (NAUX ** -0.25), 0.625, ((0, 4), (1, 4))),
        "valid_columns": ragged_sizes(part_splits[1], NOCC, (NOCC + 1) * DOM * VBW // 2, DOM * VBW, 0).astype(jnp.int32),
        "domain_blocks": draw_domain_blocks(jax.random.fold_in(jax.random.fold_in(key_list[7], part), 71), part),
        "occupied_energy": jnp.clip(-2.0 + 1.7 * jax.random.uniform(part_splits[3], (NOCC,), jnp.float32) ** levels(part_splits[3], (NOCC,), ((0, 4),), -0.2, 0.2), -2.0, -0.3),
        "virtual_energy": jnp.clip(jax.random.uniform(part_splits[4], (NVIR,), jnp.float32, 0.2, 3.0), 0.2, 3.0),
        "shell_index": jnp.searchsorted(jnp.cumsum(ragged_sizes(key_list[5], NSHELL, NAUX, 9, 0)), jnp.arange(NAUX), side="right").astype(jnp.int32),
        "centre_weights": centred(part_splits[6], (3, NAUX), 0.25, 1.5, ((1, 4),), jnp.float32),
    }


opposite_scale = 1.3


def reference(three_index, valid_columns, domain_blocks, occupied_energy, virtual_energy, shell_index, centre_weights):
    domain_width = DOM * VBW
    column = jnp.arange(domain_width, dtype=jnp.int32)
    active = column[None, :] < valid_columns[:, None]
    masked = jnp.where(active[:, None, :], three_index, jnp.zeros((), three_index.dtype))
    energy_table = virtual_energy.reshape(VB, VBW)
    virtual = energy_table[domain_blocks].reshape(NOCC, domain_width)

    def one_block(inputs):
        slab_tiles, occupied, virtual_rows = inputs
        wide = slab_tiles.astype(jnp.float32)
        grouped = wide.reshape(OCC_DEV, N_AUX * N_REP, ROWS_DEV, domain_width)
        partial_value = jnp.einsum('igpa,jgpb->gaijb', grouped, grouped)
        rounded = lax.optimization_barrier(partial_value.astype(jnp.bfloat16)).astype(jnp.float32)
        coulomb = jnp.sum(rounded, axis=0)
        denominator = (virtual_rows.T[:, :, None, None] + virtual_rows[None, None, :, :]
                       - occupied[None, :, None, None] - occupied[None, None, :, None])
        amplitudes = (opposite_scale * coulomb / denominator).astype(jnp.bfloat16)
        gamma = jnp.einsum('jpb,aijb->ipa', wide, amplitudes.astype(jnp.float32))
        weight = jnp.sum(gamma * wide, axis=(0, 2))
        return gamma.astype(jnp.bfloat16), weight

    gammas, weights = lax.map(one_block, (masked.reshape(N_OCC, OCC_DEV, NAUX, domain_width),
                                          occupied_energy.reshape(N_OCC, OCC_DEV),
                                          virtual.reshape(N_OCC, OCC_DEV, domain_width)))
    aux_weight = jnp.sum(weights, axis=0)
    terms = (centre_weights * aux_weight[None, :]).T
    shell_gradient = jax.ops.segment_sum(terms, shell_index, num_segments=NSHELL).T
    return gammas.reshape(NOCC, NAUX, domain_width), shell_gradient
```

```python
import functools
import jax
import jax.numpy as jnp
from jax import lax
from jax.experimental import pallas as pl
from jax.experimental.pallas import tpu as pltpu
from jax.sharding import PartitionSpec as P

VBW = 128
DOM = 2
WID = VBW * DOM
PACK = WID + 16
LANES = 128
OPPOSITE_SCALE = 1.3
F32 = jnp.float32
BF16 = jnp.bfloat16


def iota(shape, dim):
    return lax.broadcasted_iota(jnp.int32, shape, dim)


def tdot(x, y):
    return lax.dot_general(x, y, (((0,), (0,)), ((), ())), preferred_element_type=F32)


def gram_kernel(chunks, rank, valid, blocks, occupied, energies, three, send, keep, factor, held, sems):
    rows = three.shape[1]
    step = rows // chunks
    copies = []
    for k in range(chunks):
        part = pl.ds(k * step, step)
        copies.append(pltpu.make_async_copy(three.at[:, part, :], held.at[:, part, :], sems.at[k]))
        copies[-1].start()

    second = rank[0] == 1
    virtual = [
        jnp.concatenate([energies[pl.ds(blocks[i, d], 1), :] for d in range(DOM)], axis=1) for i in range(2)
    ]
    columns = jnp.concatenate([jnp.broadcast_to(v, (8, WID)) for v in virtual], axis=0).T
    down = [columns[:, 0:1], columns[:, 8:9]]
    a, b = iota((WID, WID), 0), iota((WID, WID), 1)
    upper = a <= b
    e0, e1 = occupied[0], occupied[1]
    v0, v1 = valid[0], valid[1]

    @pl.when(jnp.logical_not(second))
    def _():
        denominator = down[0] + virtual[1] - e0 - e1
        inside = (a < v0) & (b < v1)
        factor[0:WID, :] = jnp.where(inside, OPPOSITE_SCALE / denominator, 0.0)
        factor[WID:PACK, :] = jnp.zeros((PACK - WID, WID), F32)

    @pl.when(second)
    def _():
        denominator = jnp.where(upper, down[0] + virtual[0] - e0 - e0, down[1] + virtual[1] - e1 - e1)
        limit = jnp.where(upper, v0, v1)
        inside = (a < limit) & (b < limit)
        factor[0:WID, :] = jnp.where(inside, OPPOSITE_SCALE / denominator, 0.0)
        diagonal = jnp.broadcast_to(virtual[1] + virtual[1] - e1 - e1, (PACK - WID, WID))
        inside = iota((PACK - WID, WID), 1) < v1
        factor[WID:PACK, :] = jnp.where(inside, OPPOSITE_SCALE / diagonal, 0.0)

    c00 = c01 = c11 = None
    for k in range(chunks):
        copies[k].wait()
        b0, b1 = held[0, pl.ds(k * step, step), :], held[1, pl.ds(k * step, step), :]
        if k == 0:
            c00, c01, c11 = tdot(b0, b0), tdot(b0, b1), tdot(b1, b1)
        else:
            c00, c01, c11 = c00 + tdot(b0, b0), c01 + tdot(b0, b1), c11 + tdot(b1, b1)
    packed = jnp.where(upper, c00, c11)
    diagonal = jnp.sum(jnp.where(a == b, c11, 0.0), axis=0, keepdims=True)
    diagonal = jnp.broadcast_to(diagonal, (PACK - WID, WID))

    @pl.when(jnp.logical_not(second))
    def _():
        keep[0:WID, :] = c01
        keep[WID:PACK, :] = jnp.zeros((PACK - WID, WID), F32)
        send[0:WID, :] = packed.astype(BF16)
        send[WID:PACK, :] = diagonal.astype(BF16)

    @pl.when(second)
    def _():
        keep[0:WID, :] = packed
        keep[WID:PACK, :] = diagonal
        send[0:WID, :] = c01.astype(BF16)
        send[WID:PACK, :] = jnp.zeros((PACK - WID, WID), BF16)


def gamma_kernel(per, window, rank, firsts, own, other, three, index, weights, gamma, terms, table, padded, out, sems):
    rows = three.shape[1]
    first = rank[0] == 0
    part0 = jnp.where(first, own[...], other[...]).astype(F32)
    part1 = jnp.where(first, other[...], own[...]).astype(F32)
    a, b = iota((WID, WID), 0), iota((WID, WID), 1)
    t01 = part0[0:WID, :]
    packed = part1[0:WID, :]
    turned = packed.T
    diagonal = part1[WID : WID + 1, :]
    table[0:WID, 0:WID] = jnp.where(a <= b, packed, turned).astype(BF16)
    table[0:WID, WID : 2 * WID] = t01.astype(BF16)
    table[WID : 2 * WID, 0:WID] = t01.T.astype(BF16)
    table[WID : 2 * WID, WID : 2 * WID] = jnp.where(a > b, packed, jnp.where(a == b, diagonal, turned)).astype(BF16)
    padded[...] = jnp.zeros(padded.shape, F32)
    padded[0:3, :] = weights[...]
    terms[...] = jnp.zeros(terms.shape, F32)

    copies = []
    for k in range(rows // LANES):
        part = pl.ds(k * LANES, LANES)
        both = jnp.concatenate([three[0, part, :], three[1, part, :]], axis=1)
        g = jnp.dot(both, table[...], preferred_element_type=F32)
        out[0, part, :] = g[:, 0:WID].astype(BF16)
        out[1, part, :] = g[:, WID:].astype(BF16)
        copies.append(pltpu.make_async_copy(out.at[:, part, :], gamma.at[:, part, :], sems.at[k]))
        copies[-1].start()
        product = g * both.astype(F32)
        partial = sum(product[:, j * LANES : (j + 1) * LANES] for j in range(2 * WID // LANES))
        weight = jnp.sum(partial.T, axis=0, keepdims=True)
        term = padded[:, part] * weight
        high = term.astype(BF16)
        low = (term - high.astype(F32)).astype(BF16)
        stacked = jnp.concatenate([high.astype(F32), low.astype(F32)], axis=0).astype(BF16)
        chunk = firsts[k * LANES] // per
        relative = index[k : k + 1, :] - chunk * per
        column = relative
        for j in range(1, window):
            column = column + jnp.where(relative >= j * per, LANES - per, 0)
        hot = (iota((window * LANES, LANES), 0) == column).astype(F32).astype(BF16)
        sums = lax.dot_general(stacked, hot, (((1,), (1,)), ((), ())), preferred_element_type=F32)
        sums = sums[0:8, :] + sums[8:16, :]
        for j in range(window):
            terms[chunk + j] += sums[:, j * LANES : (j + 1) * LANES]
    for copy in copies:
        copy.wait()


def swap(x, axis, bit):
    count = lax.axis_size(axis)
    return lax.ppermute(x, axis, [(i, i ^ bit) for i in range(count)])


def shards(
    three_index,
    valid_columns,
    domain_blocks,
    occupied_energy,
    virtual_energy,
    shell_index,
    centre_weights,
    *,
    shells,
):
    rows = three_index.shape[1]
    n_occ, n_aux, n_rep = lax.axis_size("occ"), lax.axis_size("aux"), lax.axis_size("rep")
    owners = n_occ * n_aux * n_rep
    per = shells // owners
    window = (per + LANES - 2) // per + 1
    blocks = rows // LANES
    chunks = 3
    rank = lax.axis_index("rep").astype(jnp.int32).reshape(1)
    vmem = pl.BlockSpec(memory_space=pltpu.VMEM)
    smem = pl.BlockSpec(memory_space=pltpu.SMEM)
    anywhere = pl.BlockSpec(memory_space=pl.ANY)

    send, keep, factor = pl.pallas_call(
        functools.partial(gram_kernel, chunks),
        out_shape=(
            jax.ShapeDtypeStruct((PACK, WID), BF16),
            jax.ShapeDtypeStruct((PACK, WID), F32),
            jax.ShapeDtypeStruct((PACK, WID), F32),
        ),
        in_specs=[smem, smem, smem, smem, vmem, anywhere],
        out_specs=(vmem, vmem, vmem),
        scratch_shapes=[pltpu.VMEM(three_index.shape, BF16), pltpu.SemaphoreType.DMA((chunks,))],
        compiler_params=pltpu.CompilerParams(vmem_limit_bytes=16 << 20),
        name="gram",
    )(rank, valid_columns, domain_blocks, occupied_energy, virtual_energy.reshape(-1, VBW), three_index)

    sums = keep + swap(send, "rep", 1).astype(F32)
    bit = 1
    while bit < n_aux:
        sums = sums + swap(sums.astype(BF16), "aux", bit).astype(F32)
        bit *= 2
    own = (sums * factor).astype(BF16)
    other = swap(own, "rep", 1)

    gamma, terms = pl.pallas_call(
        functools.partial(gamma_kernel, per, window),
        out_shape=(
            jax.ShapeDtypeStruct(three_index.shape, BF16),
            jax.ShapeDtypeStruct((owners + window, 8, LANES), F32),
        ),
        in_specs=[smem, smem, vmem, vmem, vmem, vmem, vmem],
        out_specs=(anywhere, vmem),
        scratch_shapes=[
            pltpu.VMEM((2 * WID, 2 * WID), BF16),
            pltpu.VMEM((8, rows), F32),
            pltpu.VMEM(three_index.shape, BF16),
            pltpu.SemaphoreType.DMA((blocks,)),
        ],
        compiler_params=pltpu.CompilerParams(vmem_limit_bytes=24 << 20),
        name="gamma",
    )(rank, shell_index, own, other, three_index, shell_index.reshape(blocks, LANES), centre_weights)

    part = terms[:owners]
    for axis, count in (("occ", n_occ), ("aux", n_aux), ("rep", n_rep)):
        me = lax.axis_index(axis)
        bit = count // 2
        while bit:
            half = part.shape[0] // 2
            up = (me // bit) % 2
            mine = lax.dynamic_slice_in_dim(part, up * half, half, 0)
            theirs = lax.dynamic_slice_in_dim(part, (1 - up) * half, half, 0)
            part = mine + swap(theirs, axis, bit)
            bit //= 2
    return gamma, part[0, :3, :per]


def solution(mesh):

    def whole(three_index, valid_columns, domain_blocks, occupied_energy, virtual_energy, shell_index, centre_weights):
        shells = three_index.shape[1] // 5
        return jax.shard_map(
            functools.partial(shards, shells=shells),
            mesh=mesh,
            in_specs=(
                P(("pose", "occ"), ("aux", "rep"), None),
                P(("pose", "occ")),
                P(("pose", "occ"), None),
                P(("pose", "occ")),
                P("pose"),
                P(("aux", "rep")),
                P(None, ("pose", "aux", "rep")),
            ),
            out_specs=(
                P(("pose", "occ"), ("aux", "rep"), None),
                P(None, ("pose", "occ", "aux", "rep")),
            ),
            check_vma=False,
        )(three_index, valid_columns, domain_blocks, occupied_energy, virtual_energy, shell_index, centre_weights)

    return whole
```

```python
import functools
import jax
import jax.numpy as jnp
from jax import lax
from jax.experimental import pallas as pl
from jax.experimental.pallas import tpu as pltpu
from jax.sharding import PartitionSpec as P

VBW = 128
DOM = 2
WID = VBW * DOM
PACK = WID + 16
LANES = 128
SEG = 256
OPPOSITE_SCALE = 1.3
F32 = jnp.float32
BF16 = jnp.bfloat16


def iota(shape, dim):
    return lax.broadcasted_iota(jnp.int32, shape, dim)


def tdot(x, y):
    return lax.dot_general(x, y, (((0,), (0,)), ((), ())), preferred_element_type=F32)


def factor_kernel(valid, blocks, occupied, energies, factor):
    second = lax.axis_index("rep") == 1
    virtual = [
        jnp.concatenate([energies[pl.ds(blocks[i, d], 1), :] for d in range(DOM)], axis=1) for i in range(2)
    ]
    columns = jnp.concatenate([jnp.broadcast_to(v, (8, WID)) for v in virtual], axis=0).T
    down = [columns[:, 0:1], columns[:, 8:9]]
    a, b = iota((WID, WID), 0), iota((WID, WID), 1)
    upper = a <= b
    e0, e1 = occupied[0], occupied[1]
    v0, v1 = valid[0], valid[1]

    @pl.when(jnp.logical_not(second))
    def _():
        denominator = down[0] + virtual[1] - e0 - e1
        inside = (a < v0) & (b < v1)
        factor[0:WID, :] = jnp.where(inside, OPPOSITE_SCALE / denominator, 0.0)
        factor[WID:PACK, :] = jnp.zeros((PACK - WID, WID), F32)

    @pl.when(second)
    def _():
        denominator = jnp.where(upper, down[0] + virtual[0] - e0 - e0, down[1] + virtual[1] - e1 - e1)
        limit = jnp.where(upper, v0, v1)
        inside = (a < limit) & (b < limit)
        factor[0:WID, :] = jnp.where(inside, OPPOSITE_SCALE / denominator, 0.0)
        diagonal = jnp.broadcast_to(virtual[1] + virtual[1] - e1 - e1, (PACK - WID, WID))
        inside = iota((PACK - WID, WID), 1) < v1
        factor[WID:PACK, :] = jnp.where(inside, OPPOSITE_SCALE / diagonal, 0.0)


def gram_kernel(three, send, keep, held, sems):
    copies = [pltpu.make_async_copy(three.at[i], held.at[i], sems.at[i]) for i in range(2)]
    for copy in copies:
        copy.start()
    second = lax.axis_index("rep") == 1
    a, b = iota((WID, WID), 0), iota((WID, WID), 1)
    copies[0].wait()
    b0 = held[0]
    c00 = tdot(b0, b0)
    copies[1].wait()
    b1 = held[1]
    c01, c11 = tdot(b0, b1), tdot(b1, b1)
    packed = jnp.where(a <= b, c00, c11)
    diagonal = jnp.sum(jnp.where(a == b, c11, 0.0), axis=0, keepdims=True)
    diagonal = jnp.broadcast_to(diagonal, (PACK - WID, WID))

    @pl.when(jnp.logical_not(second))
    def _():
        keep[0:WID, :] = c01
        keep[WID:PACK, :] = jnp.zeros((PACK - WID, WID), F32)
        send[0:WID, :] = packed.astype(BF16)
        send[WID:PACK, :] = diagonal.astype(BF16)

    @pl.when(second)
    def _():
        keep[0:WID, :] = packed
        keep[WID:PACK, :] = diagonal
        send[0:WID, :] = c01.astype(BF16)
        send[WID:PACK, :] = jnp.zeros((PACK - WID, WID), BF16)


def prep_kernel(per, window, firsts, index, weights, hot, padded):
    padded[...] = jnp.zeros(padded.shape, F32)
    padded[0:3, :] = weights[...]
    lanes = iota((LANES, LANES), 1)
    for k in range(index.shape[0]):
        chunk = lax.div(firsts[k * LANES // SEG * SEG], per)
        relative = index[k : k + 1, :] - chunk * per
        column = relative
        for j in range(1, window):
            column = column + jnp.where(relative >= j * per, LANES - per, 0)
        turned = jnp.broadcast_to(column.astype(F32), (LANES, LANES)).T.astype(jnp.int32)
        for j in range(window):
            hot[pl.ds(k * LANES, LANES), pl.ds(j * LANES, LANES)] = (
                (turned == lanes + j * LANES).astype(F32).astype(BF16)
            )


def parts_of(own, other):
    first = lax.axis_index("rep") == 0
    return jnp.where(first, own[...], other[...]), jnp.where(first, other[...], own[...])


def weight_kernel(per, window, step, firsts, own, other, three, hot, padded, packs, stacked, terms):
    rows = three.shape[1]
    part0, part1 = parts_of(own, other)
    a, b = iota((WID, WID), 0), iota((WID, WID), 1)
    packed = part1[0:WID, :].astype(F32)
    diagonal = part1[WID : WID + 1, :].astype(F32)
    q00 = jnp.where(a < b, 2.0 * packed, jnp.where(a == b, packed, 0.0)).astype(BF16)
    q01 = (2.0 * part0[0:WID, :].astype(F32)).astype(BF16)
    q11 = jnp.where(a > b, 2.0 * packed, jnp.where(a == b, diagonal, 0.0)).astype(BF16)
    wide = jnp.concatenate([q00, q01], axis=1)
    terms[...] = jnp.zeros(terms.shape, F32)
    for k in range(rows // step):
        part = pl.ds(k * step, step)
        b0, b1 = three[0, part, :], three[1, part, :]
        left = jnp.dot(b0, wide, preferred_element_type=F32)
        right = jnp.dot(b1, q11, preferred_element_type=F32)
        product = left[:, 0:WID] * b0.astype(F32) + (left[:, WID:] + right) * b1.astype(F32)
        partial = product[:, 0:LANES] + product[:, LANES:WID]
        for q in range(step // LANES):
            weight = jnp.sum(partial[q * LANES : (q + 1) * LANES].T, axis=0, keepdims=True)
            lanes = pl.ds(k * step + q * LANES, LANES)
            term = padded[:, lanes] * weight
            high = term.astype(BF16).astype(F32)
            stacked[:, lanes] = jnp.concatenate([high, term - high], axis=0).astype(BF16)
    starts = range(0, rows, SEG)
    sums = []
    for start in starts:
        part = pl.ds(start, min(SEG, rows - start))
        both = jnp.dot(stacked[:, part], hot[part, :], preferred_element_type=F32)
        sums.append(both[0:8, :] + both[8:16, :])
    for start, value in zip(starts, sums):
        chunk = lax.div(firsts[start], per)
        for j in range(window):
            terms[chunk + j] += value[:, j * LANES : (j + 1) * LANES]
    for pair in range(packs.shape[0]):
        packs[pair, 0:4, :] = terms[2 * pair, 0:4, :]
        packs[pair, 4:8, :] = terms[2 * pair + 1, 0:4, :]


def gamma_kernel(begin, step, own, other, three, mine, *rest):
    gamma, kept, table, out, sems = rest[-5:]
    kept[...] = mine[...]
    part0, part1 = parts_of(own, other)
    a, b = iota((WID, WID), 0), iota((WID, WID), 1)
    t01 = part0[0:WID, :]
    packed = part1[0:WID, :]
    turned = packed.T.astype(F32)
    packed = packed.astype(F32)
    diagonal = part1[WID : WID + 1, :].astype(F32)
    table[0:WID, 0:WID] = jnp.where(a <= b, packed, turned).astype(BF16)
    table[0:WID, WID : 2 * WID] = t01
    table[WID : 2 * WID, 0:WID] = t01.T
    table[WID : 2 * WID, WID : 2 * WID] = jnp.where(a > b, packed, jnp.where(a == b, diagonal, turned)).astype(BF16)
    copies = []
    for k in range(out.shape[1] // step):
        source, target = pl.ds(begin + k * step, step), pl.ds(k * step, step)
        both = jnp.concatenate([three[0, source, :], three[1, source, :]], axis=1)
        g = jnp.dot(both, table[...], preferred_element_type=F32)
        out[0, target, :] = g[:, 0:WID].astype(BF16)
        out[1, target, :] = g[:, WID:].astype(BF16)
        copies.append(pltpu.make_async_copy(out.at[:, target, :], gamma.at[:, source, :], sems.at[k]))
        copies[-1].start()
    for copy in copies:
        copy.wait()


def swap(x, axis, bit):
    count = lax.axis_size(axis)
    return lax.ppermute(x, axis, [(i, i ^ bit) for i in range(count)])


def shards(
    three_index,
    valid_columns,
    domain_blocks,
    occupied_energy,
    virtual_energy,
    shell_index,
    centre_weights,
    *,
    shells,
):
    rows = three_index.shape[1]
    n_occ, n_aux, n_rep = lax.axis_size("occ"), lax.axis_size("aux"), lax.axis_size("rep")
    owners = n_occ * n_aux * n_rep
    per = shells // owners
    window = (per + SEG - 2) // per + 1
    vmem = pl.BlockSpec(memory_space=pltpu.VMEM)
    smem = pl.BlockSpec(memory_space=pltpu.SMEM)
    hbm = pl.BlockSpec(memory_space=pltpu.HBM)
    anywhere = pl.BlockSpec(memory_space=pl.ANY)

    def grant(mib):
        return pltpu.CompilerParams(vmem_limit_bytes=mib << 20)

    def cost(flops, size):
        return pl.CostEstimate(flops=flops, bytes_accessed=size, transcendentals=0)

    send, keep = pl.pallas_call(
        gram_kernel,
        out_shape=(jax.ShapeDtypeStruct((PACK, WID), BF16), jax.ShapeDtypeStruct((PACK, WID), F32)),
        in_specs=[hbm],
        out_specs=(vmem, vmem),
        scratch_shapes=[pltpu.VMEM(three_index.shape, BF16), pltpu.SemaphoreType.DMA((2,))],
        compiler_params=grant(52),
        cost_estimate=cost(6 * WID * WID * rows, 4 * WID * rows),
        name="gram",
    )(three_index)
    factor = pl.pallas_call(
        factor_kernel,
        out_shape=jax.ShapeDtypeStruct((PACK, WID), F32),
        in_specs=[smem, smem, smem, vmem],
        out_specs=vmem,
        compiler_params=grant(8),
        cost_estimate=cost(20 * WID * WID, 8 * WID * WID),
        name="factor",
    )(valid_columns, domain_blocks, occupied_energy, virtual_energy.reshape(-1, VBW))
    hot, padded = pl.pallas_call(
        functools.partial(prep_kernel, per, window),
        out_shape=(
            jax.ShapeDtypeStruct((rows, window * LANES), BF16),
            jax.ShapeDtypeStruct((8, rows), F32),
        ),
        in_specs=[smem, vmem, vmem],
        out_specs=(vmem, vmem),
        compiler_params=grant(12),
        cost_estimate=cost(4 * rows * window * LANES, 2 * rows * window * LANES),
        name="prep",
    )(shell_index, shell_index.reshape(-1, LANES), centre_weights)

    sums = keep + swap(send, "rep", 1).astype(F32)
    bit = 1
    while bit < n_aux:
        sums = sums + swap(sums.astype(BF16), "aux", bit).astype(F32)
        bit *= 2
    own = (sums * factor).astype(BF16)
    other = swap(own, "rep", 1)

    part = pl.pallas_call(
        functools.partial(weight_kernel, per, window, rows // 3),
        out_shape=jax.ShapeDtypeStruct((owners // 2, 8, LANES), F32),
        in_specs=[smem, vmem, vmem, vmem, vmem, vmem],
        out_specs=vmem,
        scratch_shapes=[pltpu.VMEM((16, rows), BF16), pltpu.VMEM((owners + window, 8, LANES), F32)],
        compiler_params=grant(16),
        cost_estimate=cost(6 * WID * WID * rows, 4 * WID * rows),
        name="weight",
    )(shell_index, own, other, three_index, hot, padded)

    steps = []
    for axis, count in (("occ", n_occ), ("aux", n_aux)):
        bit = count // 2
        while bit:
            steps.append((axis, bit))
            bit //= 2
    gamma = None
    pieces = 3
    for number, (axis, bit) in enumerate(steps):
        half = part.shape[0] // 2
        up = (lax.axis_index(axis) // bit) % 2
        mine = lax.dynamic_slice_in_dim(part, up * half, half, 0)
        theirs = lax.dynamic_slice_in_dim(part, (1 - up) * half, half, 0)
        if number < pieces:
            size = rows // pieces
            before = () if gamma is None else (gamma,)
            gamma, mine = pl.pallas_call(
                functools.partial(gamma_kernel, number * size, size // 2),
                out_shape=(
                    jax.ShapeDtypeStruct(three_index.shape, BF16),
                    jax.ShapeDtypeStruct(mine.shape, F32),
                ),
                in_specs=[vmem] * 4 + [hbm] * len(before),
                out_specs=(hbm, vmem),
                input_output_aliases={4: 0} if before else {},
                scratch_shapes=[
                    pltpu.VMEM((2 * WID, 2 * WID), BF16),
                    pltpu.VMEM((2, size, WID), BF16),
                    pltpu.SemaphoreType.DMA((2,)),
                ],
                compiler_params=grant(12),
                cost_estimate=cost(8 * WID * WID * size, 6 * WID * size),
                name="gamma",
            )(own, other, three_index, mine, *before)
        part = mine + swap(theirs, axis, bit)
    part = part[0] + swap(part, "rep", 1)[0]
    shell_gradient = lax.dynamic_slice(part, (4 * lax.axis_index("rep"), 0), (3, per))
    return gamma, shell_gradient


def solution(mesh):

    def whole(three_index, valid_columns, domain_blocks, occupied_energy, virtual_energy, shell_index, centre_weights):
        shells = three_index.shape[1] // 5
        return jax.shard_map(
            functools.partial(shards, shells=shells),
            mesh=mesh,
            in_specs=(
                P(("pose", "occ"), ("aux", "rep"), None),
                P(("pose", "occ")),
                P(("pose", "occ"), None),
                P(("pose", "occ")),
                P("pose"),
                P(("aux", "rep")),
                P(None, ("pose", "aux", "rep")),
            ),
            out_specs=(
                P(("pose", "occ"), ("aux", "rep"), None),
                P(None, ("pose", "occ", "aux", "rep")),
            ),
            check_vma=False,
        )(three_index, valid_columns, domain_blocks, occupied_energy, virtual_energy, shell_index, centre_weights)

    return whole
```

```python
import functools
import jax
import jax.numpy as jnp
from jax import lax
from jax.experimental import pallas as pl
from jax.experimental.pallas import tpu as pltpu
from jax.sharding import PartitionSpec as P

VBW = 128
DOM = 2
WID = VBW * DOM
PACK = WID + 16
LANES = 128
SEG = 256
OPPOSITE_SCALE = 1.3
F32 = jnp.float32
BF16 = jnp.bfloat16


def iota(shape, dim):
    return lax.broadcasted_iota(jnp.int32, shape, dim)


def tdot(x, y):
    return lax.dot_general(x, y, (((0,), (0,)), ((), ())), preferred_element_type=F32)


def make_factor(valid, blocks, occupied, energies, factor):
    second = lax.axis_index("rep") == 1
    virtual = [
        jnp.concatenate([energies[pl.ds(blocks[i, d], 1), :] for d in range(DOM)], axis=1) for i in range(2)
    ]
    columns = jnp.concatenate([jnp.broadcast_to(v, (8, WID)) for v in virtual], axis=0).T
    down = [columns[:, 0:1], columns[:, 8:9]]
    a, b = iota((WID, WID), 0), iota((WID, WID), 1)
    upper = a <= b
    e0, e1 = occupied[0], occupied[1]
    v0, v1 = valid[0], valid[1]

    @pl.when(jnp.logical_not(second))
    def _():
        denominator = down[0] + virtual[1] - e0 - e1
        inside = (a < v0) & (b < v1)
        factor[0:WID, :] = jnp.where(inside, OPPOSITE_SCALE / denominator, 0.0)
        factor[WID:PACK, :] = jnp.zeros((PACK - WID, WID), F32)

    @pl.when(second)
    def _():
        denominator = jnp.where(upper, down[0] + virtual[0] - e0 - e0, down[1] + virtual[1] - e1 - e1)
        limit = jnp.where(upper, v0, v1)
        inside = (a < limit) & (b < limit)
        factor[0:WID, :] = jnp.where(inside, OPPOSITE_SCALE / denominator, 0.0)
        diagonal = jnp.broadcast_to(virtual[1] + virtual[1] - e1 - e1, (PACK - WID, WID))
        inside = iota((PACK - WID, WID), 1) < v1
        factor[WID:PACK, :] = jnp.where(inside, OPPOSITE_SCALE / diagonal, 0.0)


def gram_part(second, pieces, held, out, ready=lambda k: None):
    step = held.shape[1] // pieces

    def total(pairs):
        sums = None
        for k in range(pieces):
            ready(k)
            rows = pl.ds(k * step, step)
            terms = [tdot(held[i, rows, :], held[j, rows, :]) for i, j in pairs]
            sums = terms if sums is None else [x + y for x, y in zip(sums, terms)]
        return sums

    @pl.when(jnp.logical_not(second))
    def _():
        (c01,) = total([(0, 1)])
        out[0:WID, :] = c01.astype(out.dtype)
        out[WID:PACK, :] = jnp.zeros((PACK - WID, WID), out.dtype)

    @pl.when(second)
    def _():
        a, b = iota((WID, WID), 0), iota((WID, WID), 1)
        c00, c11 = total([(0, 0), (1, 1)])
        diagonal = jnp.sum(jnp.where(a == b, c11, 0.0), axis=0, keepdims=True)
        out[0:WID, :] = jnp.where(a <= b, c00, c11).astype(out.dtype)
        out[WID:PACK, :] = jnp.broadcast_to(diagonal, (PACK - WID, WID)).astype(out.dtype)


def send_kernel(pieces, three, send, held, sems):
    step = three.shape[1] // pieces
    copies = []
    for k in range(pieces):
        rows = pl.ds(k * step, step)
        copies.append(pltpu.make_async_copy(three.at[:, rows, :], held.at[:, rows, :], sems.at[k]))
        copies[-1].start()
    gram_part(lax.axis_index("rep") == 0, pieces, held, send, lambda k: copies[k].wait())


def keep_kernel(held, keep):
    gram_part(lax.axis_index("rep") == 1, 1, held, keep)


def prep_kernel(
    per, window, valid, blocks, occupied, energies, firsts, index, weights, factor, columns, padded, starts
):
    make_factor(valid, blocks, occupied, energies, factor)
    padded[...] = jnp.zeros(padded.shape, F32)
    padded[0:3, :] = weights[...]
    for k in range(index.shape[0]):
        block = k * LANES // SEG
        chunk = lax.div(firsts[block * SEG], per)
        starts[block : block + 1, :] = jnp.full((1, LANES), chunk, jnp.int32)
        relative = index[k : k + 1, :] - chunk * per
        column = relative
        for j in range(1, window):
            column = column + jnp.where(relative >= j * per, LANES - per, 0)
        columns[k : k + 1, :] = column


def parts_of(own, other):
    first = lax.axis_index("rep") == 0
    return jnp.where(first, own[...], other[...]), jnp.where(first, other[...], own[...])


def quadratic(second, part, three, step, emit):
    blocks = range(0, three.shape[1], step)
    a, b = iota((WID, WID), 0), iota((WID, WID), 1)

    @pl.when(jnp.logical_not(second))
    def _():
        form = (2.0 * part[0:WID, :].astype(F32)).astype(BF16)
        for k in blocks:
            b0, b1 = three[0, pl.ds(k, step), :], three[1, pl.ds(k, step), :]
            product = jnp.dot(b0, form, preferred_element_type=F32) * b1.astype(F32)
            emit(k, product[:, 0:LANES] + product[:, LANES:WID])

    @pl.when(second)
    def _():
        packed = part[0:WID, :].astype(F32)
        diagonal = part[WID:PACK, :].astype(F32)[0:1, :]
        form0 = jnp.where(a < b, 2.0 * packed, jnp.where(a == b, packed, 0.0)).astype(BF16)
        form1 = jnp.where(a > b, 2.0 * packed, jnp.where(a == b, diagonal, 0.0)).astype(BF16)
        for k in blocks:
            b0, b1 = three[0, pl.ds(k, step), :], three[1, pl.ds(k, step), :]
            product = jnp.dot(b0, form0, preferred_element_type=F32) * b0.astype(F32)
            product += jnp.dot(b1, form1, preferred_element_type=F32) * b1.astype(F32)
            emit(k, product[:, 0:LANES] + product[:, LANES:WID])


def ahead_kernel(step, window, own, three, columns, ahead, hot):
    lanes = iota((LANES, LANES), 1)
    for k in range(columns.shape[0]):
        turned = jnp.broadcast_to(columns[k : k + 1, :].astype(F32), (LANES, LANES)).T.astype(jnp.int32)
        for j in range(window):
            hot[pl.ds(k * LANES, LANES), pl.ds(j * LANES, LANES)] = (
                (turned == lanes + j * LANES).astype(F32).astype(BF16)
            )

    def emit(k, partial):
        ahead[pl.ds(k, step), :] = partial

    quadratic(lax.axis_index("rep") == 1, own, three, step, emit)


def weight_kernel(window, step, starts, other, ahead, three, hot, padded, packs, stacked, terms, chunks, sem):
    rows = three.shape[1]
    copy = pltpu.make_async_copy(starts, chunks, sem)
    copy.start()
    terms[...] = jnp.zeros(terms.shape, F32)

    def emit(k, partial):
        partial = partial + ahead[pl.ds(k, step), :]
        for q in range(0, step, LANES):
            weight = jnp.sum(partial[q : q + LANES].T, axis=0, keepdims=True)
            lanes = pl.ds(k + q, LANES)
            term = padded[:, lanes] * weight
            high = term.astype(BF16).astype(F32)
            stacked[:, lanes] = jnp.concatenate([high, term - high], axis=0).astype(BF16)

    quadratic(lax.axis_index("rep") == 0, other, three, step, emit)
    sums = []
    for start in range(0, rows, SEG):
        part = pl.ds(start, min(SEG, rows - start))
        both = jnp.dot(stacked[:, part], hot[part, :], preferred_element_type=F32)
        sums.append(both[0:8, :] + both[8:16, :])
    copy.wait()
    for block, value in enumerate(sums):
        chunk = chunks[block, 0]
        for j in range(window):
            terms[chunk + j] += value[:, j * LANES : (j + 1) * LANES]
    for pair in range(packs.shape[0]):
        packs[pair, 0:4, :] = terms[2 * pair, 0:4, :]
        packs[pair, 4:8, :] = terms[2 * pair + 1, 0:4, :]


def gamma_kernel(begin, step, own, other, three, mine, *rest):
    gamma, kept, table, out, sems = rest[-5:]
    kept[...] = mine[...]
    part0, part1 = parts_of(own, other)
    a, b = iota((WID, WID), 0), iota((WID, WID), 1)
    t01 = part0[0:WID, :]
    packed = part1[0:WID, :]
    turned = packed.T.astype(F32)
    packed = packed.astype(F32)
    diagonal = part1[WID : WID + 1, :].astype(F32)
    table[0:WID, 0:WID] = jnp.where(a <= b, packed, turned).astype(BF16)
    table[0:WID, WID : 2 * WID] = t01
    table[WID : 2 * WID, 0:WID] = t01.T
    table[WID : 2 * WID, WID : 2 * WID] = jnp.where(a > b, packed, jnp.where(a == b, diagonal, turned)).astype(BF16)
    copies = []
    for k in range(out.shape[1] // step):
        source, target = pl.ds(begin + k * step, step), pl.ds(k * step, step)
        both = jnp.concatenate([three[0, source, :], three[1, source, :]], axis=1)
        g = jnp.dot(both, table[...], preferred_element_type=F32)
        out[0, target, :] = g[:, 0:WID].astype(BF16)
        out[1, target, :] = g[:, WID:].astype(BF16)
        copies.append(pltpu.make_async_copy(out.at[:, target, :], gamma.at[:, source, :], sems.at[k]))
        copies[-1].start()
    for copy in copies:
        copy.wait()


def swap(x, axis, bit):
    count = lax.axis_size(axis)
    return lax.ppermute(x, axis, [(i, i ^ bit) for i in range(count)])


def shards(
    three_index,
    valid_columns,
    domain_blocks,
    occupied_energy,
    virtual_energy,
    shell_index,
    centre_weights,
    *,
    shells,
):
    rows = three_index.shape[1]
    n_occ, n_aux, n_rep = lax.axis_size("occ"), lax.axis_size("aux"), lax.axis_size("rep")
    owners = n_occ * n_aux * n_rep
    per = shells // owners
    window = (per + SEG - 2) // per + 1
    vmem = pl.BlockSpec(memory_space=pltpu.VMEM)
    smem = pl.BlockSpec(memory_space=pltpu.SMEM)
    hbm = pl.BlockSpec(memory_space=pltpu.HBM)
    anywhere = pl.BlockSpec(memory_space=pl.ANY)

    def grant(mib):
        return pltpu.CompilerParams(vmem_limit_bytes=mib << 20)

    def cost(flops, size):
        return pl.CostEstimate(flops=flops, bytes_accessed=size, transcendentals=0)

    send, held = pl.pallas_call(
        functools.partial(send_kernel, 4),
        out_shape=(jax.ShapeDtypeStruct((PACK, WID), BF16), jax.ShapeDtypeStruct(three_index.shape, BF16)),
        in_specs=[hbm],
        out_specs=(vmem, vmem),
        scratch_shapes=[pltpu.SemaphoreType.DMA((4,))],
        compiler_params=grant(51),
        cost_estimate=cost(4 * WID * WID * rows, 4 * WID * rows),
        name="send",
    )(three_index)
    keep = pl.pallas_call(
        keep_kernel,
        out_shape=jax.ShapeDtypeStruct((PACK, WID), F32),
        in_specs=[vmem],
        out_specs=vmem,
        compiler_params=grant(16),
        cost_estimate=cost(4 * WID * WID * rows, 4 * WID * rows),
        name="keep",
    )(held)
    factor, columns, padded, starts = pl.pallas_call(
        functools.partial(prep_kernel, per, window),
        out_shape=(
            jax.ShapeDtypeStruct((PACK, WID), F32),
            jax.ShapeDtypeStruct((rows // LANES, LANES), jnp.int32),
            jax.ShapeDtypeStruct((8, rows), F32),
            jax.ShapeDtypeStruct((8, LANES), jnp.int32),
        ),
        in_specs=[smem, smem, smem, vmem, smem, vmem, vmem],
        out_specs=(vmem,) * 4,
        compiler_params=grant(16),
        cost_estimate=cost(4 * rows * window * LANES, 2 * rows * window * LANES),
        name="prep",
    )(
        valid_columns,
        domain_blocks,
        occupied_energy,
        virtual_energy.reshape(-1, VBW),
        shell_index,
        shell_index.reshape(-1, LANES),
        centre_weights,
    )

    sums = keep + swap(send, "rep", 1).astype(F32)
    bit = 1
    while bit < n_aux:
        sums = sums + swap(sums.astype(BF16), "aux", bit).astype(F32)
        bit *= 2
    own = (sums * factor).astype(BF16)
    other = swap(own, "rep", 1)

    step = rows // 3
    ahead, hot = pl.pallas_call(
        functools.partial(ahead_kernel, step, window),
        out_shape=(
            jax.ShapeDtypeStruct((rows, LANES), F32),
            jax.ShapeDtypeStruct((rows, window * LANES), BF16),
        ),
        in_specs=[vmem] * 3,
        out_specs=(vmem, vmem),
        compiler_params=grant(16),
        cost_estimate=cost(4 * WID * WID * rows, 4 * WID * rows),
        name="ahead",
    )(own, held, columns)
    part = pl.pallas_call(
        functools.partial(weight_kernel, window, step),
        out_shape=jax.ShapeDtypeStruct((owners // 2, 8, LANES), F32),
        in_specs=[vmem] * 6,
        out_specs=vmem,
        scratch_shapes=[
            pltpu.VMEM((16, rows), BF16),
            pltpu.VMEM((owners + window, 8, LANES), F32),
            pltpu.SMEM((8, LANES), jnp.int32),
            pltpu.SemaphoreType.DMA,
        ],
        compiler_params=grant(16),
        cost_estimate=cost(4 * WID * WID * rows, 4 * WID * rows),
        name="weight",
    )(starts, other, ahead, held, hot, padded)

    steps = []
    for axis, count in (("occ", n_occ), ("aux", n_aux)):
        bit = count // 2
        while bit:
            steps.append((axis, bit))
            bit //= 2
    gamma = None
    pieces = 3
    for number, (axis, bit) in enumerate(steps):
        half = part.shape[0] // 2
        up = (lax.axis_index(axis) // bit) % 2
        mine = lax.dynamic_slice_in_dim(part, up * half, half, 0)
        theirs = lax.dynamic_slice_in_dim(part, (1 - up) * half, half, 0)
        if number < pieces:
            size = rows // pieces
            before = () if gamma is None else (gamma,)
            gamma, mine = pl.pallas_call(
                functools.partial(gamma_kernel, number * size, size // 2),
                out_shape=(
                    jax.ShapeDtypeStruct(three_index.shape, BF16),
                    jax.ShapeDtypeStruct(mine.shape, F32),
                ),
                in_specs=[vmem] * 4 + [hbm] * len(before),
                out_specs=(hbm, vmem),
                input_output_aliases={4: 0} if before else {},
                scratch_shapes=[
                    pltpu.VMEM((2 * WID, 2 * WID), BF16),
                    pltpu.VMEM((2, size, WID), BF16),
                    pltpu.SemaphoreType.DMA((2,)),
                ],
                compiler_params=grant(12),
                cost_estimate=cost(8 * WID * WID * size, 6 * WID * size),
                name="gamma",
            )(own, other, held, mine, *before)
        part = mine + swap(theirs, axis, bit)
    part = part[0] + swap(part, "rep", 1)[0]
    shell_gradient = lax.dynamic_slice(part, (4 * lax.axis_index("rep"), 0), (3, per))
    return gamma, shell_gradient


def solution(mesh):

    def whole(three_index, valid_columns, domain_blocks, occupied_energy, virtual_energy, shell_index, centre_weights):
        shells = three_index.shape[1] // 5
        return jax.shard_map(
            functools.partial(shards, shells=shells),
            mesh=mesh,
            in_specs=(
                P(("pose", "occ"), ("aux", "rep"), None),
                P(("pose", "occ")),
                P(("pose", "occ"), None),
                P(("pose", "occ")),
                P("pose"),
                P(("aux", "rep")),
                P(None, ("pose", "aux", "rep")),
            ),
            out_specs=(
                P(("pose", "occ"), ("aux", "rep"), None),
                P(None, ("pose", "occ", "aux", "rep")),
            ),
            check_vma=False,
        )(three_index, valid_columns, domain_blocks, occupied_energy, virtual_energy, shell_index, centre_weights)

    return whole
```

```python
import functools
import jax
import jax.numpy as jnp
from jax import lax
from jax.experimental import pallas as pl
from jax.experimental.pallas import tpu as pltpu
from jax.sharding import PartitionSpec as P

VBW = 128
DOM = 2
WID = VBW * DOM
PACK = WID + 16
LANES = 128
SEG = 256
SIZES = (960, 960)
OPPOSITE_SCALE = 1.3
F32 = jnp.float32
BF16 = jnp.bfloat16


def iota(shape, dim):
    return lax.broadcasted_iota(jnp.int32, shape, dim)


def tdot(x, y):
    return lax.dot_general(x, y, (((0,), (0,)), ((), ())), preferred_element_type=F32)


def make_factor(valid, blocks, occupied, energies, factor):
    second = lax.axis_index("rep") == 1
    virtual = [
        jnp.concatenate([energies[pl.ds(blocks[i, d], 1), :] for d in range(DOM)], axis=1) for i in range(2)
    ]
    columns = jnp.concatenate([jnp.broadcast_to(v, (8, WID)) for v in virtual], axis=0).T
    down = [columns[:, 0:1], columns[:, 8:9]]
    a, b = iota((WID, WID), 0), iota((WID, WID), 1)
    upper = a <= b
    e0, e1 = occupied[0], occupied[1]
    v0, v1 = valid[0], valid[1]

    @pl.when(jnp.logical_not(second))
    def _():
        denominator = down[0] + virtual[1] - e0 - e1
        inside = (a < v0) & (b < v1)
        factor[0:WID, :] = jnp.where(inside, OPPOSITE_SCALE / denominator, 0.0)
        factor[WID:PACK, :] = jnp.zeros((PACK - WID, WID), F32)

    @pl.when(second)
    def _():
        denominator = jnp.where(upper, down[0] + virtual[0] - e0 - e0, down[1] + virtual[1] - e1 - e1)
        limit = jnp.where(upper, v0, v1)
        inside = (a < limit) & (b < limit)
        factor[0:WID, :] = jnp.where(inside, OPPOSITE_SCALE / denominator, 0.0)
        diagonal = jnp.broadcast_to(virtual[1] + virtual[1] - e1 - e1, (PACK - WID, WID))
        inside = iota((PACK - WID, WID), 1) < v1
        factor[WID:PACK, :] = jnp.where(inside, OPPOSITE_SCALE / diagonal, 0.0)


def gram_part(second, pieces, held, out, ready=lambda k: None):
    step = held.shape[1] // pieces

    def total(pairs):
        sums = None
        for k in range(pieces):
            ready(k)
            rows = pl.ds(k * step, step)
            terms = [tdot(held[i, rows, :], held[j, rows, :]) for i, j in pairs]
            sums = terms if sums is None else [x + y for x, y in zip(sums, terms)]
        return sums

    @pl.when(jnp.logical_not(second))
    def _():
        (c01,) = total([(0, 1)])
        out[0:WID, :] = c01.astype(out.dtype)
        out[WID:PACK, :] = jnp.zeros((PACK - WID, WID), out.dtype)

    @pl.when(second)
    def _():
        a, b = iota((WID, WID), 0), iota((WID, WID), 1)
        c00, c11 = total([(0, 0), (1, 1)])
        diagonal = jnp.sum(jnp.where(a == b, c11, 0.0), axis=0, keepdims=True)
        out[0:WID, :] = jnp.where(a <= b, c00, c11).astype(out.dtype)
        out[WID:PACK, :] = jnp.broadcast_to(diagonal, (PACK - WID, WID)).astype(out.dtype)


def send_kernel(pieces, three, send, held, sems):
    step = three.shape[1] // pieces
    copies = []
    for k in range(pieces):
        rows = pl.ds(k * step, step)
        copies.append(pltpu.make_async_copy(three.at[:, rows, :], held.at[:, rows, :], sems.at[k]))
        copies[-1].start()
    gram_part(lax.axis_index("rep") == 0, pieces, held, send, lambda k: copies[k].wait())


def keep_kernel(held, keep):
    gram_part(lax.axis_index("rep") == 1, 1, held, keep)


def prep_kernel(
    per, window, valid, blocks, occupied, energies, firsts, index, weights, factor, columns, padded, starts
):
    make_factor(valid, blocks, occupied, energies, factor)
    padded[...] = jnp.zeros(padded.shape, F32)
    padded[0:3, :] = weights[...]
    for k in range(index.shape[0]):
        block = k * LANES // SEG
        chunk = lax.div(firsts[block * SEG], per)
        starts[block : block + 1, :] = jnp.full((1, LANES), chunk, jnp.int32)
        relative = index[k : k + 1, :] - chunk * per
        column = relative
        for j in range(1, window):
            column = column + jnp.where(relative >= j * per, LANES - per, 0)
        columns[k : k + 1, :] = column


def parts_of(own, other):
    first = lax.axis_index("rep") == 0
    return jnp.where(first, own[...], other[...]), jnp.where(first, other[...], own[...])


def quadratic(second, part, three, step, emit):
    blocks = range(0, three.shape[1], step)
    a, b = iota((WID, WID), 0), iota((WID, WID), 1)

    @pl.when(jnp.logical_not(second))
    def _():
        form = (2.0 * part[0:WID, :].astype(F32)).astype(BF16)
        for k in blocks:
            b0, b1 = three[0, pl.ds(k, step), :], three[1, pl.ds(k, step), :]
            product = jnp.dot(b0, form, preferred_element_type=F32) * b1.astype(F32)
            emit(k, product[:, 0:LANES] + product[:, LANES:WID])

    @pl.when(second)
    def _():
        packed = part[0:WID, :].astype(F32)
        diagonal = part[WID:PACK, :].astype(F32)[0:1, :]
        form0 = jnp.where(a < b, 2.0 * packed, jnp.where(a == b, packed, 0.0)).astype(BF16)
        form1 = jnp.where(a > b, 2.0 * packed, jnp.where(a == b, diagonal, 0.0)).astype(BF16)
        for k in blocks:
            b0, b1 = three[0, pl.ds(k, step), :], three[1, pl.ds(k, step), :]
            product = jnp.dot(b0, form0, preferred_element_type=F32) * b0.astype(F32)
            product += jnp.dot(b1, form1, preferred_element_type=F32) * b1.astype(F32)
            emit(k, product[:, 0:LANES] + product[:, LANES:WID])


def ahead_kernel(step, window, own, three, columns, ahead, hot):
    lanes = iota((LANES, LANES), 1)
    for k in range(columns.shape[0]):
        turned = jnp.broadcast_to(columns[k : k + 1, :].astype(F32), (LANES, LANES)).T.astype(jnp.int32)
        for j in range(window):
            hot[pl.ds(k * LANES, LANES), pl.ds(j * LANES, LANES)] = (
                (turned == lanes + j * LANES).astype(F32).astype(BF16)
            )

    def emit(k, partial):
        ahead[pl.ds(k, step), :] = partial

    quadratic(lax.axis_index("rep") == 1, own, three, step, emit)


def weight_kernel(window, step, starts, other, ahead, three, hot, padded, packs, stacked, terms, chunks, sem):
    rows = three.shape[1]
    copy = pltpu.make_async_copy(starts, chunks, sem)
    copy.start()
    terms[...] = jnp.zeros(terms.shape, F32)

    def emit(k, partial):
        partial = partial + ahead[pl.ds(k, step), :]
        for q in range(0, step, LANES):
            weight = jnp.sum(partial[q : q + LANES].T, axis=0, keepdims=True)
            lanes = pl.ds(k + q, LANES)
            term = padded[:, lanes] * weight
            high = term.astype(BF16).astype(F32)
            stacked[:, lanes] = jnp.concatenate([high, term - high], axis=0).astype(BF16)

    quadratic(lax.axis_index("rep") == 0, other, three, step, emit)
    sums = []
    for start in range(0, rows, SEG):
        part = pl.ds(start, min(SEG, rows - start))
        both = jnp.dot(stacked[:, part], hot[part, :], preferred_element_type=F32)
        sums.append(both[0:8, :] + both[8:16, :])
    copy.wait()
    for block, value in enumerate(sums):
        chunk = chunks[block, 0]
        for j in range(window):
            terms[chunk + j] += value[:, j * LANES : (j + 1) * LANES]
    for pair in range(packs.shape[0]):
        packs[pair, 0:4, :] = terms[2 * pair, 0:4, :]
        packs[pair, 4:8, :] = terms[2 * pair + 1, 0:4, :]


def gamma_kernel(begin, step, own, other, three, mine, *rest):
    gamma, kept, table, out, sems = rest[-5:]
    kept[...] = mine[...]
    part0, part1 = parts_of(own, other)
    a, b = iota((WID, WID), 0), iota((WID, WID), 1)
    t01 = part0[0:WID, :]
    packed = part1[0:WID, :]
    turned = packed.T.astype(F32)
    packed = packed.astype(F32)
    diagonal = part1[WID : WID + 1, :].astype(F32)
    table[0:WID, 0:WID] = jnp.where(a <= b, packed, turned).astype(BF16)
    table[0:WID, WID : 2 * WID] = t01
    table[WID : 2 * WID, 0:WID] = t01.T
    table[WID : 2 * WID, WID : 2 * WID] = jnp.where(a > b, packed, jnp.where(a == b, diagonal, turned)).astype(BF16)
    copies = []
    for k in range(out.shape[1] // step):
        source, target = pl.ds(begin + k * step, step), pl.ds(k * step, step)
        both = jnp.concatenate([three[0, source, :], three[1, source, :]], axis=1)
        g = jnp.dot(both, table[...], preferred_element_type=F32)
        out[0, target, :] = g[:, 0:WID].astype(BF16)
        out[1, target, :] = g[:, WID:].astype(BF16)
        copies.append(pltpu.make_async_copy(out.at[:, target, :], gamma.at[:, source, :], sems.at[k]))
        copies[-1].start()
    for copy in copies:
        copy.wait()


def swap(x, axis, bit):
    count = lax.axis_size(axis)
    return lax.ppermute(x, axis, [(i, i ^ bit) for i in range(count)])


def shards(
    three_index,
    valid_columns,
    domain_blocks,
    occupied_energy,
    virtual_energy,
    shell_index,
    centre_weights,
    *,
    shells,
):
    rows = three_index.shape[1]
    n_occ, n_aux, n_rep = lax.axis_size("occ"), lax.axis_size("aux"), lax.axis_size("rep")
    owners = n_occ * n_aux * n_rep
    per = shells // owners
    window = (per + SEG - 2) // per + 1
    vmem = pl.BlockSpec(memory_space=pltpu.VMEM)
    smem = pl.BlockSpec(memory_space=pltpu.SMEM)
    hbm = pl.BlockSpec(memory_space=pltpu.HBM)
    anywhere = pl.BlockSpec(memory_space=pl.ANY)

    def grant(mib):
        return pltpu.CompilerParams(vmem_limit_bytes=mib << 20)

    def cost(flops, size):
        return pl.CostEstimate(flops=flops, bytes_accessed=size, transcendentals=0)

    send, held = pl.pallas_call(
        functools.partial(send_kernel, 4),
        out_shape=(jax.ShapeDtypeStruct((PACK, WID), BF16), jax.ShapeDtypeStruct(three_index.shape, BF16)),
        in_specs=[hbm],
        out_specs=(vmem, vmem),
        scratch_shapes=[pltpu.SemaphoreType.DMA((4,))],
        compiler_params=grant(51),
        cost_estimate=cost(4 * WID * WID * rows, 4 * WID * rows),
        name="send",
    )(three_index)
    keep = pl.pallas_call(
        keep_kernel,
        out_shape=jax.ShapeDtypeStruct((PACK, WID), F32),
        in_specs=[vmem],
        out_specs=vmem,
        compiler_params=grant(16),
        cost_estimate=cost(4 * WID * WID * rows, 4 * WID * rows),
        name="keep",
    )(held)
    factor, columns, padded, starts = pl.pallas_call(
        functools.partial(prep_kernel, per, window),
        out_shape=(
            jax.ShapeDtypeStruct((PACK, WID), F32),
            jax.ShapeDtypeStruct((rows // LANES, LANES), jnp.int32),
            jax.ShapeDtypeStruct((8, rows), F32),
            jax.ShapeDtypeStruct((8, LANES), jnp.int32),
        ),
        in_specs=[smem, smem, smem, vmem, smem, vmem, vmem],
        out_specs=(vmem,) * 4,
        compiler_params=grant(16),
        cost_estimate=cost(4 * rows * window * LANES, 2 * rows * window * LANES),
        name="prep",
    )(
        valid_columns,
        domain_blocks,
        occupied_energy,
        virtual_energy.reshape(-1, VBW),
        shell_index,
        shell_index.reshape(-1, LANES),
        centre_weights,
    )

    sums = keep + swap(send, "rep", 1).astype(F32)
    bit = 1
    while bit < n_aux:
        sums = sums + swap(sums.astype(BF16), "aux", bit).astype(F32)
        bit *= 2
    own = (sums * factor).astype(BF16)
    other = swap(own, "rep", 1)

    step = rows // 3
    ahead, hot = pl.pallas_call(
        functools.partial(ahead_kernel, step, window),
        out_shape=(
            jax.ShapeDtypeStruct((rows, LANES), F32),
            jax.ShapeDtypeStruct((rows, window * LANES), BF16),
        ),
        in_specs=[vmem] * 3,
        out_specs=(vmem, vmem),
        compiler_params=grant(16),
        cost_estimate=cost(4 * WID * WID * rows, 4 * WID * rows),
        name="ahead",
    )(own, held, columns)
    part = pl.pallas_call(
        functools.partial(weight_kernel, window, step),
        out_shape=jax.ShapeDtypeStruct((owners // 2, 8, LANES), F32),
        in_specs=[vmem] * 6,
        out_specs=vmem,
        scratch_shapes=[
            pltpu.VMEM((16, rows), BF16),
            pltpu.VMEM((owners + window, 8, LANES), F32),
            pltpu.SMEM((8, LANES), jnp.int32),
            pltpu.SemaphoreType.DMA,
        ],
        compiler_params=grant(16),
        cost_estimate=cost(4 * WID * WID * rows, 4 * WID * rows),
        name="weight",
    )(starts, other, ahead, held, hot, padded)

    gamma = None
    begin = 0

    def beside(size, mine):
        nonlocal gamma, begin
        if not size:
            return mine
        before = () if gamma is None else (gamma,)
        gamma, mine = pl.pallas_call(
            functools.partial(gamma_kernel, begin, size // 3),
            out_shape=(jax.ShapeDtypeStruct(three_index.shape, BF16), jax.ShapeDtypeStruct(mine.shape, F32)),
            in_specs=[vmem] * 4 + [hbm] * len(before),
            out_specs=(hbm, vmem),
            input_output_aliases={4: 0} if before else {},
            scratch_shapes=[
                pltpu.VMEM((2 * WID, 2 * WID), BF16),
                pltpu.VMEM((2, size, WID), BF16),
                pltpu.SemaphoreType.DMA((3,)),
            ],
            compiler_params=grant(12),
            cost_estimate=cost(8 * WID * WID * size, 6 * WID * size),
            name="gamma",
        )(own, other, held, mine, *before)
        begin += size
        return mine

    def block(x, index, count=1):
        return lax.dynamic_slice_in_dim(x, index * count, count, 0)

    place, core = lax.axis_index("occ"), lax.axis_index("rep")
    part = part.reshape(n_occ, n_aux, 8, LANES)
    bit = n_occ // 2
    while bit > 2:
        half = part.shape[0] // 2
        up = (place // bit) % 2
        part = block(part, up, half) + swap(block(part, 1 - up, half), "occ", bit)
        bit //= 2

    low = place % 4
    first = core == 0
    far, near = jnp.where(first, low ^ 3, low ^ 2), jnp.where(first, low, low ^ 1)
    its_far, its_near = jnp.where(first, low ^ 2, low ^ 3), jnp.where(first, low ^ 1, low)
    mine = jnp.concatenate([block(part, far), block(part, near)], axis=0)
    mine_sums = mine + swap(jnp.concatenate([block(part, its_far), block(part, its_near)], axis=0), "rep", 1)
    across = [(2 * i + r, 2 * (i ^ (3 - r)) + r) for i in range(n_occ) for r in range(2)]
    beside_it = [(2 * i + 1, 2 * (i ^ 1) + 1) for i in range(n_occ)]
    received = lax.ppermute(mine_sums[0], ("occ", "rep"), across)
    received1 = lax.ppermute(mine_sums[1], ("occ", "rep"), beside_it)
    kept = beside(SIZES[0], mine_sums[1])
    part = received + jnp.where(first, kept, received1)

    sizes = list(SIZES[1:])
    bit = n_aux // 2
    while bit:
        half = part.shape[0] // 2
        up = (lax.axis_index("aux") // bit) % 2
        mine = beside(sizes.pop(0) if sizes else 0, block(part, up, half))
        part = mine + swap(block(part, 1 - up, half), "aux", bit)
        bit //= 2
    part = part[0] + swap(part, "rep", 1)[0]
    shell_gradient = lax.dynamic_slice(part, (4 * core, 0), (3, per))
    return gamma, shell_gradient


def solution(mesh):

    def whole(three_index, valid_columns, domain_blocks, occupied_energy, virtual_energy, shell_index, centre_weights):
        shells = three_index.shape[1] // 5
        return jax.shard_map(
            functools.partial(shards, shells=shells),
            mesh=mesh,
            in_specs=(
                P(("pose", "occ"), ("aux", "rep"), None),
                P(("pose", "occ")),
                P(("pose", "occ"), None),
                P(("pose", "occ")),
                P("pose"),
                P(("aux", "rep")),
                P(None, ("pose", "aux", "rep")),
            ),
            out_specs=(
                P(("pose", "occ"), ("aux", "rep"), None),
                P(None, ("pose", "occ", "aux", "rep")),
            ),
            check_vma=False,
        )(three_index, valid_columns, domain_blocks, occupied_energy, virtual_energy, shell_index, centre_weights)

    return whole
```

```python
import functools
import jax
import jax.numpy as jnp
from jax import lax
from jax.experimental import pallas as pl
from jax.experimental.pallas import tpu as pltpu
from jax.sharding import PartitionSpec as P

VBW = 128
DOM = 2
WID = VBW * DOM
PACK = WID + 16
LANES = 128
SEG = 128
SIZES = (960, 960)
PACKED = 0
PIECES = (1280, 640)
OPPOSITE_SCALE = 1.3
F32 = jnp.float32
BF16 = jnp.bfloat16


def iota(shape, dim):
    return lax.broadcasted_iota(jnp.int32, shape, dim)


def slices(sizes):
    return [pl.ds(sum(sizes[:k]), size) for k, size in enumerate(sizes)]


def tdot(x, y):
    return lax.dot_general(x, y, (((0,), (0,)), ((), ())), preferred_element_type=F32)


def make_factor(valid, blocks, occupied, energies, factor):
    second = lax.axis_index("rep") == PACKED
    virtual = [
        jnp.concatenate([energies[pl.ds(blocks[i, d], 1), :] for d in range(DOM)], axis=1) for i in range(2)
    ]
    columns = jnp.concatenate([jnp.broadcast_to(v, (8, WID)) for v in virtual], axis=0).T
    down = [columns[:, 0:1], columns[:, 8:9]]
    a, b = iota((WID, WID), 0), iota((WID, WID), 1)
    upper = a <= b
    e0, e1 = occupied[0], occupied[1]
    v0, v1 = valid[0], valid[1]

    @pl.when(jnp.logical_not(second))
    def _():
        denominator = down[0] + virtual[1] - e0 - e1
        inside = (a < v0) & (b < v1)
        factor[0:WID, :] = jnp.where(inside, OPPOSITE_SCALE / denominator, 0.0)
        factor[WID:PACK, :] = jnp.zeros((PACK - WID, WID), F32)

    @pl.when(second)
    def _():
        denominator = jnp.where(upper, down[0] + virtual[0] - e0 - e0, down[1] + virtual[1] - e1 - e1)
        limit = jnp.where(upper, v0, v1)
        inside = (a < limit) & (b < limit)
        factor[0:WID, :] = jnp.where(inside, OPPOSITE_SCALE / denominator, 0.0)
        diagonal = jnp.broadcast_to(virtual[1] + virtual[1] - e1 - e1, (PACK - WID, WID))
        inside = iota((PACK - WID, WID), 1) < v1
        factor[WID:PACK, :] = jnp.where(inside, OPPOSITE_SCALE / diagonal, 0.0)


def gram_part(second, pieces, held, out, ready=lambda k: None):
    def total(pairs):
        sums = None
        for k, rows in enumerate(slices(pieces)):
            ready(k)
            terms = [tdot(held[i, rows, :], held[j, rows, :]) for i, j in pairs]
            sums = terms if sums is None else [x + y for x, y in zip(sums, terms)]
        return sums

    @pl.when(jnp.logical_not(second))
    def _():
        (c01,) = total([(0, 1)])
        out[0:WID, :] = c01.astype(out.dtype)
        out[WID:PACK, :] = jnp.zeros((PACK - WID, WID), out.dtype)

    @pl.when(second)
    def _():
        a, b = iota((WID, WID), 0), iota((WID, WID), 1)
        c00, c11 = total([(0, 0), (1, 1)])
        diagonal = jnp.sum(jnp.where(a == b, c11, 0.0), axis=0, keepdims=True)
        out[0:WID, :] = jnp.where(a <= b, c00, c11).astype(out.dtype)
        out[WID:PACK, :] = jnp.broadcast_to(diagonal, (PACK - WID, WID)).astype(out.dtype)


def send_kernel(pieces, three, send, held, sems):
    copies = []
    for k, rows in enumerate(slices(pieces)):
        copies.append(pltpu.make_async_copy(three.at[:, rows, :], held.at[:, rows, :], sems.at[k]))
        copies[-1].start()
    gram_part(lax.axis_index("rep") != PACKED, pieces, held, send, lambda k: copies[k].wait())


def keep_kernel(held, keep):
    gram_part(lax.axis_index("rep") == PACKED, [held.shape[1]], held, keep)


def prep_kernel(
    window, valid, blocks, occupied, energies, firsts, index, weights, factor, hot, padded, starts
):
    make_factor(valid, blocks, occupied, energies, factor)
    padded[...] = jnp.zeros(padded.shape, F32)
    padded[0:3, :] = weights[...]
    lanes = iota((LANES, LANES), 1)
    for k in range(index.shape[0]):
        block = k * LANES // SEG
        tile = lax.div(firsts[block * SEG], LANES)
        starts[block : block + 1, :] = jnp.full((1, LANES), tile, jnp.int32)
        column = index[k : k + 1, :] - tile * LANES
        turned = jnp.broadcast_to(column.astype(F32), (LANES, LANES)).T.astype(jnp.int32)
        for j in range(window):
            hot[pl.ds(k * LANES, LANES), pl.ds(j * LANES, LANES)] = (
                (turned == lanes + j * LANES).astype(F32).astype(BF16)
            )


def parts_of(own, other):
    first = lax.axis_index("rep") != PACKED
    return jnp.where(first, own[...], other[...]), jnp.where(first, other[...], own[...])


def quadratic(second, part, three, step, emit):
    blocks = range(0, three.shape[1], step)
    a, b = iota((WID, WID), 0), iota((WID, WID), 1)

    @pl.when(jnp.logical_not(second))
    def _():
        form = (2.0 * part[0:WID, :].astype(F32)).astype(BF16)
        for k in blocks:
            b0, b1 = three[0, pl.ds(k, step), :], three[1, pl.ds(k, step), :]
            product = jnp.dot(b0, form, preferred_element_type=F32) * b1.astype(F32)
            emit(k, product[:, 0:LANES] + product[:, LANES:WID])

    @pl.when(second)
    def _():
        packed = part[0:WID, :].astype(F32)
        diagonal = part[WID:PACK, :].astype(F32)[0:1, :]
        form0 = jnp.where(a < b, 2.0 * packed, jnp.where(a == b, packed, 0.0)).astype(BF16)
        form1 = jnp.where(a > b, 2.0 * packed, jnp.where(a == b, diagonal, 0.0)).astype(BF16)
        for k in blocks:
            b0, b1 = three[0, pl.ds(k, step), :], three[1, pl.ds(k, step), :]
            product = jnp.dot(b0, form0, preferred_element_type=F32) * b0.astype(F32)
            product += jnp.dot(b1, form1, preferred_element_type=F32) * b1.astype(F32)
            emit(k, product[:, 0:LANES] + product[:, LANES:WID])


def ahead_kernel(step, own, three, ahead):
    def emit(k, partial):
        ahead[pl.ds(k, step), :] = partial

    quadratic(lax.axis_index("rep") == PACKED, own, three, step, emit)


def weight_kernel(window, per, step, starts, other, ahead, three, hot, padded, packs, sums, terms, tops, sem):
    rows = three.shape[1]
    copy = pltpu.make_async_copy(starts, tops, sem)
    copy.start()
    terms[...] = jnp.zeros(terms.shape, F32)

    def emit(k, partial):
        partial = partial + ahead[pl.ds(k, step), :]
        for q in range(0, step, LANES):
            weight = jnp.sum(partial[q : q + LANES].T, axis=0, keepdims=True)
            lanes = pl.ds(k + q, LANES)
            term = padded[:, lanes] * weight
            high = term.astype(BF16).astype(F32)
            stacked = jnp.concatenate([high, term - high], axis=0).astype(BF16)
            both = jnp.dot(stacked, hot[lanes, :], preferred_element_type=F32)
            sums[(k + q) // LANES] = both[0:8, :] + both[8:16, :]

    quadratic(lax.axis_index("rep") != PACKED, other, three, step, emit)
    copy.wait()
    for block in range(rows // LANES):
        value = sums[block]
        tile = tops[block, 0]
        for j in range(window):
            terms[tile + j] += value[:, j * LANES : (j + 1) * LANES]
    for owner in range(2 * packs.shape[0]):
        tile, lane = owner * per // LANES, owner * per % LANES
        value = terms[tile]
        if lane:
            value = pltpu.roll(value, LANES - lane, 1)
        if lane + per > LANES:
            value = jnp.where(iota(value.shape, 1) < LANES - lane, value, pltpu.roll(terms[tile + 1], LANES - lane, 1))
        packs[owner // 2, owner % 2 * 4 : owner % 2 * 4 + 4, :] = value[0:4, :]


def gamma_kernel(begin, step, own, other, three, mine, *rest):
    gamma, kept, table, out, sems = rest[-5:]
    kept[...] = mine[...]
    part0, part1 = parts_of(own, other)
    a, b = iota((WID, WID), 0), iota((WID, WID), 1)
    t01 = part0[0:WID, :]
    packed = part1[0:WID, :]
    turned = packed.T.astype(F32)
    packed = packed.astype(F32)
    diagonal = part1[WID : WID + 1, :].astype(F32)
    table[0:WID, 0:WID] = jnp.where(a <= b, packed, turned).astype(BF16)
    table[0:WID, WID : 2 * WID] = t01
    table[WID : 2 * WID, 0:WID] = t01.T
    table[WID : 2 * WID, WID : 2 * WID] = jnp.where(a > b, packed, jnp.where(a == b, diagonal, turned)).astype(BF16)
    copies = []
    for k in range(out.shape[1] // step):
        source, target = pl.ds(begin + k * step, step), pl.ds(k * step, step)
        both = jnp.concatenate([three[0, source, :], three[1, source, :]], axis=1)
        g = jnp.dot(both, table[...], preferred_element_type=F32)
        out[0, target, :] = g[:, 0:WID].astype(BF16)
        out[1, target, :] = g[:, WID:].astype(BF16)
        copies.append(pltpu.make_async_copy(out.at[:, target, :], gamma.at[:, source, :], sems.at[k]))
        copies[-1].start()
    for copy in copies:
        copy.wait()


def swap(x, axis, bit):
    count = lax.axis_size(axis)
    return lax.ppermute(x, axis, [(i, i ^ bit) for i in range(count)])


def shards(
    three_index,
    valid_columns,
    domain_blocks,
    occupied_energy,
    virtual_energy,
    shell_index,
    centre_weights,
    *,
    shells,
):
    rows = three_index.shape[1]
    n_occ, n_aux, n_rep = lax.axis_size("occ"), lax.axis_size("aux"), lax.axis_size("rep")
    owners = n_occ * n_aux * n_rep
    per = shells // owners
    window = (LANES + SEG - 2) // LANES + 1
    tiles = -(-shells // LANES) + window
    vmem = pl.BlockSpec(memory_space=pltpu.VMEM)
    smem = pl.BlockSpec(memory_space=pltpu.SMEM)
    hbm = pl.BlockSpec(memory_space=pltpu.HBM)
    anywhere = pl.BlockSpec(memory_space=pl.ANY)

    def grant(mib):
        return pltpu.CompilerParams(vmem_limit_bytes=mib << 20)

    def cost(flops, size):
        return pl.CostEstimate(flops=flops, bytes_accessed=size, transcendentals=0)

    send, held = pl.pallas_call(
        functools.partial(send_kernel, PIECES),
        out_shape=(jax.ShapeDtypeStruct((PACK, WID), BF16), jax.ShapeDtypeStruct(three_index.shape, BF16)),
        in_specs=[hbm],
        out_specs=(vmem, vmem),
        scratch_shapes=[pltpu.SemaphoreType.DMA((len(PIECES),))],
        compiler_params=grant(51),
        cost_estimate=cost(4 * WID * WID * rows, 4 * WID * rows),
        name="send",
    )(three_index)
    keep = pl.pallas_call(
        keep_kernel,
        out_shape=jax.ShapeDtypeStruct((PACK, WID), F32),
        in_specs=[vmem],
        out_specs=vmem,
        compiler_params=grant(16),
        cost_estimate=cost(4 * WID * WID * rows, 4 * WID * rows),
        name="keep",
    )(held)
    factor, hot, padded, starts = pl.pallas_call(
        functools.partial(prep_kernel, window),
        out_shape=(
            jax.ShapeDtypeStruct((PACK, WID), F32),
            jax.ShapeDtypeStruct((rows, window * LANES), BF16),
            jax.ShapeDtypeStruct((8, rows), F32),
            jax.ShapeDtypeStruct((16, LANES), jnp.int32),
        ),
        in_specs=[smem, smem, smem, vmem, smem, vmem, vmem],
        out_specs=(vmem,) * 4,
        compiler_params=grant(16),
        cost_estimate=cost(4 * rows * window * LANES, 2 * rows * window * LANES),
        name="prep",
    )(
        valid_columns,
        domain_blocks,
        occupied_energy,
        virtual_energy.reshape(-1, VBW),
        shell_index,
        shell_index.reshape(-1, LANES),
        centre_weights,
    )

    sums = keep + swap(send, "rep", 1).astype(F32)
    bit = 1
    while bit < n_aux:
        sums = sums + swap(sums.astype(BF16), "aux", bit).astype(F32)
        bit *= 2
    own = (sums * factor).astype(BF16)
    other = swap(own, "rep", 1)

    step = rows
    ahead = pl.pallas_call(
        functools.partial(ahead_kernel, step),
        out_shape=jax.ShapeDtypeStruct((rows, LANES), F32),
        in_specs=[vmem] * 2,
        out_specs=vmem,
        compiler_params=grant(16),
        cost_estimate=cost(4 * WID * WID * rows, 4 * WID * rows),
        name="ahead",
    )(own, held)
    part = pl.pallas_call(
        functools.partial(weight_kernel, window, per, step),
        out_shape=jax.ShapeDtypeStruct((owners // 2, 8, LANES), F32),
        in_specs=[vmem] * 6,
        out_specs=vmem,
        scratch_shapes=[
            pltpu.VMEM((rows // LANES, 8, window * LANES), F32),
            pltpu.VMEM((tiles, 8, LANES), F32),
            pltpu.SMEM((16, LANES), jnp.int32),
            pltpu.SemaphoreType.DMA,
        ],
        compiler_params=grant(16),
        cost_estimate=cost(4 * WID * WID * rows, 4 * WID * rows),
        name="weight",
    )(starts, other, ahead, held, hot, padded)

    gamma = None
    begin = 0

    def beside(size, mine):
        nonlocal gamma, begin
        if not size:
            return mine
        before = () if gamma is None else (gamma,)
        gamma, mine = pl.pallas_call(
            functools.partial(gamma_kernel, begin, size // 3),
            out_shape=(jax.ShapeDtypeStruct(three_index.shape, BF16), jax.ShapeDtypeStruct(mine.shape, F32)),
            in_specs=[vmem] * 4 + [hbm] * len(before),
            out_specs=(hbm, vmem),
            input_output_aliases={4: 0} if before else {},
            scratch_shapes=[
                pltpu.VMEM((2 * WID, 2 * WID), BF16),
                pltpu.VMEM((2, size, WID), BF16),
                pltpu.SemaphoreType.DMA((3,)),
            ],
            compiler_params=grant(12),
            cost_estimate=cost(8 * WID * WID * size, 6 * WID * size),
            name="gamma",
        )(own, other, held, mine, *before)
        begin += size
        return mine

    def block(x, index, count=1):
        return lax.dynamic_slice_in_dim(x, index * count, count, 0)

    place, core = lax.axis_index("occ"), lax.axis_index("rep")
    part = part.reshape(n_occ, n_aux, 8, LANES)
    bit = n_occ // 2
    while bit > 2:
        half = part.shape[0] // 2
        up = (place // bit) % 2
        part = block(part, up, half) + swap(block(part, 1 - up, half), "occ", bit)
        bit //= 2

    low = place % 4
    first = core == 0
    far, near = jnp.where(first, low ^ 3, low ^ 2), jnp.where(first, low, low ^ 1)
    its_far, its_near = jnp.where(first, low ^ 2, low ^ 3), jnp.where(first, low ^ 1, low)
    mine = jnp.concatenate([block(part, far), block(part, near)], axis=0)
    mine_sums = mine + swap(jnp.concatenate([block(part, its_far), block(part, its_near)], axis=0), "rep", 1)
    across = [(2 * i + r, 2 * (i ^ (3 - r)) + r) for i in range(n_occ) for r in range(2)]
    beside_it = [(2 * i + 1, 2 * (i ^ 1) + 1) for i in range(n_occ)]
    received = lax.ppermute(mine_sums[0], ("occ", "rep"), across)
    received1 = lax.ppermute(mine_sums[1], ("occ", "rep"), beside_it)
    kept = beside(SIZES[0], mine_sums[1])
    part = received + jnp.where(first, kept, received1)

    sizes = list(SIZES[1:])
    bit = n_aux // 2
    while bit:
        half = part.shape[0] // 2
        up = (lax.axis_index("aux") // bit) % 2
        mine = beside(sizes.pop(0) if sizes else 0, block(part, up, half))
        part = mine + swap(block(part, 1 - up, half), "aux", bit)
        bit //= 2
    part = part[0] + swap(part, "rep", 1)[0]
    shell_gradient = lax.dynamic_slice(part, (4 * core, 0), (3, per))
    return gamma, shell_gradient


def solution(mesh):

    def whole(three_index, valid_columns, domain_blocks, occupied_energy, virtual_energy, shell_index, centre_weights):
        shells = three_index.shape[1] // 5
        return jax.shard_map(
            functools.partial(shards, shells=shells),
            mesh=mesh,
            in_specs=(
                P(("pose", "occ"), ("aux", "rep"), None),
                P(("pose", "occ")),
                P(("pose", "occ"), None),
                P(("pose", "occ")),
                P("pose"),
                P(("aux", "rep")),
                P(None, ("pose", "aux", "rep")),
            ),
            out_specs=(
                P(("pose", "occ"), ("aux", "rep"), None),
                P(None, ("pose", "occ", "aux", "rep")),
            ),
            check_vma=False,
        )(three_index, valid_columns, domain_blocks, occupied_energy, virtual_energy, shell_index, centre_weights)

    return whole
```

```python
import functools
import jax
import jax.numpy as jnp
from jax import lax
from jax.experimental import pallas as pl
from jax.experimental.pallas import tpu as pltpu
from jax.sharding import PartitionSpec as P

VBW = 128
DOM = 2
WID = VBW * DOM
PACK = WID + 16
LANES = 128
SEG = 128
PACKED = 0
PIECES = (1280, 640)
OPPOSITE_SCALE = 1.3
F32 = jnp.float32
BF16 = jnp.bfloat16


def iota(shape, dim):
    return lax.broadcasted_iota(jnp.int32, shape, dim)


def slices(sizes):
    return [pl.ds(sum(sizes[:k]), size) for k, size in enumerate(sizes)]


def tdot(x, y):
    return lax.dot_general(x, y, (((0,), (0,)), ((), ())), preferred_element_type=F32)


def make_factor(valid, blocks, occupied, energies, factor):
    second = lax.axis_index("rep") == PACKED
    virtual = [
        jnp.concatenate([energies[pl.ds(blocks[i, d], 1), :] for d in range(DOM)], axis=1) for i in range(2)
    ]
    columns = jnp.concatenate([jnp.broadcast_to(v, (8, WID)) for v in virtual], axis=0).T
    down = [columns[:, 0:1], columns[:, 8:9]]
    a, b = iota((WID, WID), 0), iota((WID, WID), 1)
    upper = a <= b
    e0, e1 = occupied[0], occupied[1]
    v0, v1 = valid[0], valid[1]

    @pl.when(jnp.logical_not(second))
    def _():
        denominator = down[0] + virtual[1] - e0 - e1
        inside = (a < v0) & (b < v1)
        factor[0:WID, :] = jnp.where(inside, OPPOSITE_SCALE / denominator, 0.0)
        factor[WID:PACK, :] = jnp.zeros((PACK - WID, WID), F32)

    @pl.when(second)
    def _():
        denominator = jnp.where(upper, down[0] + virtual[0] - e0 - e0, down[1] + virtual[1] - e1 - e1)
        limit = jnp.where(upper, v0, v1)
        inside = (a < limit) & (b < limit)
        factor[0:WID, :] = jnp.where(inside, OPPOSITE_SCALE / denominator, 0.0)
        diagonal = jnp.broadcast_to(virtual[1] + virtual[1] - e1 - e1, (PACK - WID, WID))
        inside = iota((PACK - WID, WID), 1) < v1
        factor[WID:PACK, :] = jnp.where(inside, OPPOSITE_SCALE / diagonal, 0.0)


def gram_part(second, pieces, held, out, ready=lambda k: None):
    def total(pairs):
        sums = None
        for k, rows in enumerate(slices(pieces)):
            ready(k)
            terms = [tdot(held[i, rows, :], held[j, rows, :]) for i, j in pairs]
            sums = terms if sums is None else [x + y for x, y in zip(sums, terms)]
        return sums

    @pl.when(jnp.logical_not(second))
    def _():
        (c01,) = total([(0, 1)])
        out[0:WID, :] = c01.astype(out.dtype)
        out[WID:PACK, :] = jnp.zeros((PACK - WID, WID), out.dtype)

    @pl.when(second)
    def _():
        a, b = iota((WID, WID), 0), iota((WID, WID), 1)
        c00, c11 = total([(0, 0), (1, 1)])
        diagonal = jnp.sum(jnp.where(a == b, c11, 0.0), axis=0, keepdims=True)
        out[0:WID, :] = jnp.where(a <= b, c00, c11).astype(out.dtype)
        out[WID:PACK, :] = jnp.broadcast_to(diagonal, (PACK - WID, WID)).astype(out.dtype)


def send_kernel(pieces, three, send, held, sems):
    copies = []
    for k, rows in enumerate(slices(pieces)):
        copies.append(pltpu.make_async_copy(three.at[:, rows, :], held.at[:, rows, :], sems.at[k]))
        copies[-1].start()
    gram_part(lax.axis_index("rep") != PACKED, pieces, held, send, lambda k: copies[k].wait())


def keep_kernel(held, keep):
    gram_part(lax.axis_index("rep") == PACKED, [held.shape[1]], held, keep)


def prep_kernel(
    window, valid, blocks, occupied, energies, firsts, index, weights, factor, hot, padded, starts
):
    make_factor(valid, blocks, occupied, energies, factor)
    padded[...] = jnp.zeros(padded.shape, F32)
    padded[0:3, :] = weights[...]
    lanes = iota((LANES, LANES), 1)
    for k in range(index.shape[0]):
        block = k * LANES // SEG
        tile = lax.div(firsts[block * SEG], LANES)
        starts[block : block + 1, :] = jnp.full((1, LANES), tile, jnp.int32)
        column = index[k : k + 1, :] - tile * LANES
        turned = jnp.broadcast_to(column.astype(F32), (LANES, LANES)).T.astype(jnp.int32)
        for j in range(window):
            hot[pl.ds(k * LANES, LANES), pl.ds(j * LANES, LANES)] = (
                (turned == lanes + j * LANES).astype(F32).astype(BF16)
            )


def parts_of(own, other):
    first = lax.axis_index("rep") != PACKED
    return jnp.where(first, own[...], other[...]), jnp.where(first, other[...], own[...])


def quadratic(second, part, three, step, emit):
    blocks = range(0, three.shape[1], step)
    a, b = iota((WID, WID), 0), iota((WID, WID), 1)

    @pl.when(jnp.logical_not(second))
    def _():
        form = (2.0 * part[0:WID, :].astype(F32)).astype(BF16)
        for k in blocks:
            b0, b1 = three[0, pl.ds(k, step), :], three[1, pl.ds(k, step), :]
            product = jnp.dot(b0, form, preferred_element_type=F32) * b1.astype(F32)
            emit(k, product[:, 0:LANES] + product[:, LANES:WID])

    @pl.when(second)
    def _():
        packed = part[0:WID, :].astype(F32)
        diagonal = part[WID:PACK, :].astype(F32)[0:1, :]
        form0 = jnp.where(a < b, 2.0 * packed, jnp.where(a == b, packed, 0.0)).astype(BF16)
        form1 = jnp.where(a > b, 2.0 * packed, jnp.where(a == b, diagonal, 0.0)).astype(BF16)
        for k in blocks:
            b0, b1 = three[0, pl.ds(k, step), :], three[1, pl.ds(k, step), :]
            product = jnp.dot(b0, form0, preferred_element_type=F32) * b0.astype(F32)
            product += jnp.dot(b1, form1, preferred_element_type=F32) * b1.astype(F32)
            emit(k, product[:, 0:LANES] + product[:, LANES:WID])


def ahead_kernel(step, own, three, ahead):
    def emit(k, partial):
        ahead[pl.ds(k, step), :] = partial

    quadratic(lax.axis_index("rep") == PACKED, own, three, step, emit)


def weight_kernel(window, per, step, starts, other, ahead, three, hot, padded, packs, sums, terms, tops, sem):
    rows = three.shape[1]
    copy = pltpu.make_async_copy(starts, tops, sem)
    copy.start()
    terms[...] = jnp.zeros(terms.shape, F32)

    def emit(k, partial):
        partial = partial + ahead[pl.ds(k, step), :]
        for q in range(0, step, LANES):
            weight = jnp.sum(partial[q : q + LANES].T, axis=0, keepdims=True)
            lanes = pl.ds(k + q, LANES)
            term = padded[:, lanes] * weight
            high = term.astype(BF16).astype(F32)
            stacked = jnp.concatenate([high, term - high], axis=0).astype(BF16)
            both = jnp.dot(stacked, hot[lanes, :], preferred_element_type=F32)
            sums[(k + q) // LANES] = both[0:8, :] + both[8:16, :]

    quadratic(lax.axis_index("rep") != PACKED, other, three, step, emit)
    copy.wait()
    for block in range(rows // LANES):
        value = sums[block]
        tile = tops[block, 0]
        for j in range(window):
            terms[tile + j] += value[:, j * LANES : (j + 1) * LANES]
    for owner in range(2 * packs.shape[0]):
        tile, lane = owner * per // LANES, owner * per % LANES
        value = terms[tile]
        if lane:
            value = pltpu.roll(value, LANES - lane, 1)
        if lane + per > LANES:
            value = jnp.where(iota(value.shape, 1) < LANES - lane, value, pltpu.roll(terms[tile + 1], LANES - lane, 1))
        packs[owner // 2, owner % 2 * 4 : owner % 2 * 4 + 4, :] = value[0:4, :]


def gamma_rows(table, three, begin, out):
    rows = pl.ds(begin, out.shape[1])
    both = jnp.concatenate([three[0, rows, :], three[1, rows, :]], axis=1)
    g = jnp.dot(both, table[...], preferred_element_type=F32)
    out[0] = g[:, 0:WID].astype(BF16)
    out[1] = g[:, WID:].astype(BF16)


def gamma_first(own, other, three, mine, kept, table, out):
    kept[...] = mine[...]
    part0, part1 = parts_of(own, other)
    a, b = iota((WID, WID), 0), iota((WID, WID), 1)
    t01 = part0[0:WID, :]
    packed = part1[0:WID, :]
    turned = packed.T.astype(F32)
    packed = packed.astype(F32)
    diagonal = part1[WID : WID + 1, :].astype(F32)
    table[0:WID, 0:WID] = jnp.where(a <= b, packed, turned).astype(BF16)
    table[0:WID, WID : 2 * WID] = t01
    table[WID : 2 * WID, 0:WID] = t01.T
    table[WID : 2 * WID, WID : 2 * WID] = jnp.where(a > b, packed, jnp.where(a == b, diagonal, turned)).astype(BF16)
    gamma_rows(table, three, 0, out)


def gamma_second(table, three, done, mine, gamma, kept, out, sem):
    copy = pltpu.make_async_copy(done, gamma.at[:, pl.ds(0, done.shape[1]), :], sem)
    copy.start()
    kept[...] = mine[...]
    gamma_rows(table, three, done.shape[1], out)
    copy.wait()


def gamma_last(done, mine, before, gamma, kept, sem):
    copy = pltpu.make_async_copy(done, gamma.at[:, pl.ds(done.shape[1], done.shape[1]), :], sem)
    copy.start()
    kept[...] = mine[...]
    copy.wait()


def swap(x, axis, bit):
    count = lax.axis_size(axis)
    return lax.ppermute(x, axis, [(i, i ^ bit) for i in range(count)])


def shards(
    three_index,
    valid_columns,
    domain_blocks,
    occupied_energy,
    virtual_energy,
    shell_index,
    centre_weights,
    *,
    shells,
):
    rows = three_index.shape[1]
    n_occ, n_aux, n_rep = lax.axis_size("occ"), lax.axis_size("aux"), lax.axis_size("rep")
    owners = n_occ * n_aux * n_rep
    per = shells // owners
    window = (LANES + SEG - 2) // LANES + 1
    tiles = -(-shells // LANES) + window
    vmem = pl.BlockSpec(memory_space=pltpu.VMEM)
    smem = pl.BlockSpec(memory_space=pltpu.SMEM)
    hbm = pl.BlockSpec(memory_space=pltpu.HBM)
    anywhere = pl.BlockSpec(memory_space=pl.ANY)

    def grant(mib):
        return pltpu.CompilerParams(vmem_limit_bytes=mib << 20)

    def cost(flops, size):
        return pl.CostEstimate(flops=flops, bytes_accessed=size, transcendentals=0)

    send, held = pl.pallas_call(
        functools.partial(send_kernel, PIECES),
        out_shape=(jax.ShapeDtypeStruct((PACK, WID), BF16), jax.ShapeDtypeStruct(three_index.shape, BF16)),
        in_specs=[hbm],
        out_specs=(vmem, vmem),
        scratch_shapes=[pltpu.SemaphoreType.DMA((len(PIECES),))],
        compiler_params=grant(51),
        cost_estimate=cost(4 * WID * WID * rows, 4 * WID * rows),
        name="send",
    )(three_index)
    keep = pl.pallas_call(
        keep_kernel,
        out_shape=jax.ShapeDtypeStruct((PACK, WID), F32),
        in_specs=[vmem],
        out_specs=vmem,
        compiler_params=grant(16),
        cost_estimate=cost(4 * WID * WID * rows, 4 * WID * rows),
        name="keep",
    )(held)
    factor, hot, padded, starts = pl.pallas_call(
        functools.partial(prep_kernel, window),
        out_shape=(
            jax.ShapeDtypeStruct((PACK, WID), F32),
            jax.ShapeDtypeStruct((rows, window * LANES), BF16),
            jax.ShapeDtypeStruct((8, rows), F32),
            jax.ShapeDtypeStruct((16, LANES), jnp.int32),
        ),
        in_specs=[smem, smem, smem, vmem, smem, vmem, vmem],
        out_specs=(vmem,) * 4,
        compiler_params=grant(16),
        cost_estimate=cost(4 * rows * window * LANES, 2 * rows * window * LANES),
        name="prep",
    )(
        valid_columns,
        domain_blocks,
        occupied_energy,
        virtual_energy.reshape(-1, VBW),
        shell_index,
        shell_index.reshape(-1, LANES),
        centre_weights,
    )

    sums = keep + swap(send, "rep", 1).astype(F32)
    bit = 1
    while bit < n_aux:
        sums = sums + swap(sums.astype(BF16), "aux", bit).astype(F32)
        bit *= 2
    own = (sums * factor).astype(BF16)
    other = swap(own, "rep", 1)

    step = rows
    ahead = pl.pallas_call(
        functools.partial(ahead_kernel, step),
        out_shape=jax.ShapeDtypeStruct((rows, LANES), F32),
        in_specs=[vmem] * 2,
        out_specs=vmem,
        compiler_params=grant(16),
        cost_estimate=cost(4 * WID * WID * rows, 4 * WID * rows),
        name="ahead",
    )(own, held)
    part = pl.pallas_call(
        functools.partial(weight_kernel, window, per, step),
        out_shape=jax.ShapeDtypeStruct((owners // 2, 8, LANES), F32),
        in_specs=[vmem] * 6,
        out_specs=vmem,
        scratch_shapes=[
            pltpu.VMEM((rows // LANES, 8, window * LANES), F32),
            pltpu.VMEM((tiles, 8, LANES), F32),
            pltpu.SMEM((16, LANES), jnp.int32),
            pltpu.SemaphoreType.DMA,
        ],
        compiler_params=grant(16),
        cost_estimate=cost(4 * WID * WID * rows, 4 * WID * rows),
        name="weight",
    )(starts, other, ahead, held, hot, padded)

    halves = jax.ShapeDtypeStruct((2, rows // 2, WID), BF16)
    whole = jax.ShapeDtypeStruct(three_index.shape, BF16)

    def like(x):
        return jax.ShapeDtypeStruct(x.shape, x.dtype)

    def block(x, index, count=1):
        return lax.dynamic_slice_in_dim(x, index * count, count, 0)

    place, core = lax.axis_index("occ"), lax.axis_index("rep")
    part = part.reshape(n_occ, n_aux, 8, LANES)
    bit = n_occ // 2
    while bit > 2:
        half = part.shape[0] // 2
        up = (place // bit) % 2
        part = block(part, up, half) + swap(block(part, 1 - up, half), "occ", bit)
        bit //= 2

    low = place % 4
    first = core == 0
    far, near = jnp.where(first, low ^ 3, low ^ 2), jnp.where(first, low, low ^ 1)
    its_far, its_near = jnp.where(first, low ^ 2, low ^ 3), jnp.where(first, low ^ 1, low)
    mine = jnp.concatenate([block(part, far), block(part, near)], axis=0)
    mine, table, done = pl.pallas_call(
        gamma_first,
        out_shape=(like(mine), jax.ShapeDtypeStruct((2 * WID, 2 * WID), BF16), halves),
        in_specs=[vmem] * 4,
        out_specs=(vmem,) * 3,
        compiler_params=grant(12),
        cost_estimate=cost(4 * WID * WID * rows, 4 * WID * rows),
        name="gamma_first",
    )(own, other, held, mine)
    mine_sums = mine + swap(jnp.concatenate([block(part, its_far), block(part, its_near)], axis=0), "rep", 1)
    across = [(2 * i + r, 2 * (i ^ (3 - r)) + r) for i in range(n_occ) for r in range(2)]
    beside_it = [(2 * i + 1, 2 * (i ^ 1) + 1) for i in range(n_occ)]
    received = lax.ppermute(mine_sums[0], ("occ", "rep"), across)
    received1 = lax.ppermute(mine_sums[1], ("occ", "rep"), beside_it)
    gamma, kept, done = pl.pallas_call(
        gamma_second,
        out_shape=(whole, like(mine_sums[1]), halves),
        in_specs=[vmem] * 4,
        out_specs=(hbm, vmem, vmem),
        scratch_shapes=[pltpu.SemaphoreType.DMA],
        compiler_params=grant(12),
        cost_estimate=cost(4 * WID * WID * rows, 4 * WID * rows),
        name="gamma_second",
    )(table, held, done, mine_sums[1])
    part = received + jnp.where(first, kept, received1)

    bit = n_aux // 2
    while bit:
        half = part.shape[0] // 2
        up = (lax.axis_index("aux") // bit) % 2
        mine = block(part, up, half)
        if done is not None:
            gamma, mine = pl.pallas_call(
                gamma_last,
                out_shape=(whole, like(mine)),
                in_specs=[vmem, vmem, hbm],
                out_specs=(hbm, vmem),
                input_output_aliases={2: 0},
                scratch_shapes=[pltpu.SemaphoreType.DMA],
                compiler_params=grant(4),
                cost_estimate=cost(4 * WID * WID * rows, 4 * WID * rows),
                name="gamma_last",
            )(done, mine, gamma)
            done = None
        part = mine + swap(block(part, 1 - up, half), "aux", bit)
        bit //= 2
    part = part[0] + swap(part, "rep", 1)[0]
    shell_gradient = lax.dynamic_slice(part, (4 * core, 0), (3, per))
    return gamma, shell_gradient


def solution(mesh):

    def whole(three_index, valid_columns, domain_blocks, occupied_energy, virtual_energy, shell_index, centre_weights):
        shells = three_index.shape[1] // 5
        return jax.shard_map(
            functools.partial(shards, shells=shells),
            mesh=mesh,
            in_specs=(
                P(("pose", "occ"), ("aux", "rep"), None),
                P(("pose", "occ")),
                P(("pose", "occ"), None),
                P(("pose", "occ")),
                P("pose"),
                P(("aux", "rep")),
                P(None, ("pose", "aux", "rep")),
            ),
            out_specs=(
                P(("pose", "occ"), ("aux", "rep"), None),
                P(None, ("pose", "occ", "aux", "rep")),
            ),
            check_vma=False,
        )(three_index, valid_columns, domain_blocks, occupied_energy, virtual_energy, shell_index, centre_weights)

    return whole
```

```python
import functools
import jax
import jax.numpy as jnp
from jax import lax
from jax.experimental import pallas as pl
from jax.experimental.pallas import tpu as pltpu
from jax.sharding import PartitionSpec as P

VBW = 128
DOM = 2
WID = VBW * DOM
PACK = WID + 16
LANES = 128
SEG = 128
PACKED = 0
PIECES = (1280, 640)
OPPOSITE_SCALE = 1.3
F32 = jnp.float32
BF16 = jnp.bfloat16


def iota(shape, dim):
    return lax.broadcasted_iota(jnp.int32, shape, dim)


def slices(sizes):
    return [pl.ds(sum(sizes[:k]), size) for k, size in enumerate(sizes)]


def tdot(x, y):
    return lax.dot_general(x, y, (((0,), (0,)), ((), ())), preferred_element_type=F32)


def make_factor(valid, blocks, occupied, energies, factor):
    second = lax.axis_index("rep") == PACKED
    virtual = [
        jnp.concatenate([energies[pl.ds(blocks[i, d], 1), :] for d in range(DOM)], axis=1) for i in range(2)
    ]
    columns = jnp.concatenate([jnp.broadcast_to(v, (8, WID)) for v in virtual], axis=0).T
    down = [columns[:, 0:1], columns[:, 8:9]]
    a, b = iota((WID, WID), 0), iota((WID, WID), 1)
    upper = a <= b
    e0, e1 = occupied[0], occupied[1]
    v0, v1 = valid[0], valid[1]

    @pl.when(jnp.logical_not(second))
    def _():
        denominator = down[0] + virtual[1] - e0 - e1
        inside = (a < v0) & (b < v1)
        factor[0:WID, :] = jnp.where(inside, OPPOSITE_SCALE / denominator, 0.0)
        factor[WID:PACK, :] = jnp.zeros((PACK - WID, WID), F32)

    @pl.when(second)
    def _():
        denominator = jnp.where(upper, down[0] + virtual[0] - e0 - e0, down[1] + virtual[1] - e1 - e1)
        limit = jnp.where(upper, v0, v1)
        inside = (a < limit) & (b < limit)
        factor[0:WID, :] = jnp.where(inside, OPPOSITE_SCALE / denominator, 0.0)
        diagonal = jnp.broadcast_to(virtual[1] + virtual[1] - e1 - e1, (PACK - WID, WID))
        inside = iota((PACK - WID, WID), 1) < v1
        factor[WID:PACK, :] = jnp.where(inside, OPPOSITE_SCALE / diagonal, 0.0)


def gram_part(second, pieces, held, out, ready=lambda k: None):
    def total(pairs):
        sums = None
        for k, rows in enumerate(slices(pieces)):
            ready(k)
            terms = [tdot(held[i, rows, :], held[j, rows, :]) for i, j in pairs]
            sums = terms if sums is None else [x + y for x, y in zip(sums, terms)]
        return sums

    @pl.when(jnp.logical_not(second))
    def _():
        (c01,) = total([(0, 1)])
        out[0:WID, :] = c01.astype(out.dtype)
        out[WID:PACK, :] = jnp.zeros((PACK - WID, WID), out.dtype)

    @pl.when(second)
    def _():
        a, b = iota((WID, WID), 0), iota((WID, WID), 1)
        c00, c11 = total([(0, 0), (1, 1)])
        diagonal = jnp.sum(jnp.where(a == b, c11, 0.0), axis=0, keepdims=True)
        out[0:WID, :] = jnp.where(a <= b, c00, c11).astype(out.dtype)
        out[WID:PACK, :] = jnp.broadcast_to(diagonal, (PACK - WID, WID)).astype(out.dtype)


def send_kernel(pieces, three, send, held, sems):
    copies = []
    for k, rows in enumerate(slices(pieces)):
        copies.append(pltpu.make_async_copy(three.at[:, rows, :], held.at[:, rows, :], sems.at[k]))
        copies[-1].start()
    gram_part(lax.axis_index("rep") != PACKED, pieces, held, send, lambda k: copies[k].wait())


def keep_kernel(held, keep):
    gram_part(lax.axis_index("rep") == PACKED, [held.shape[1]], held, keep)


def prep_kernel(
    window, valid, blocks, occupied, energies, firsts, index, weights, factor, hot, padded, starts
):
    make_factor(valid, blocks, occupied, energies, factor)
    padded[...] = jnp.zeros(padded.shape, F32)
    padded[0:3, :] = weights[...]
    lanes = iota((LANES, LANES), 1)
    for k in range(index.shape[0]):
        block = k * LANES // SEG
        tile = lax.div(firsts[block * SEG], LANES)
        starts[block : block + 1, :] = jnp.full((1, LANES), tile, jnp.int32)
        column = index[k : k + 1, :] - tile * LANES
        turned = jnp.broadcast_to(column.astype(F32), (LANES, LANES)).T.astype(jnp.int32)
        for j in range(window):
            hot[pl.ds(k * LANES, LANES), pl.ds(j * LANES, LANES)] = (
                (turned == lanes + j * LANES).astype(F32).astype(BF16)
            )


def parts_of(own, other):
    first = lax.axis_index("rep") != PACKED
    return jnp.where(first, own[...], other[...]), jnp.where(first, other[...], own[...])


def quadratic(second, part, three, step, emit):
    blocks = range(0, three.shape[1], step)
    a, b = iota((WID, WID), 0), iota((WID, WID), 1)

    @pl.when(jnp.logical_not(second))
    def _():
        form = (2.0 * part[0:WID, :].astype(F32)).astype(BF16)
        for k in blocks:
            b0, b1 = three[0, pl.ds(k, step), :], three[1, pl.ds(k, step), :]
            product = jnp.dot(b0, form, preferred_element_type=F32) * b1.astype(F32)
            emit(k, product[:, 0:LANES] + product[:, LANES:WID])

    @pl.when(second)
    def _():
        packed = part[0:WID, :].astype(F32)
        diagonal = part[WID:PACK, :].astype(F32)[0:1, :]
        form0 = jnp.where(a < b, 2.0 * packed, jnp.where(a == b, packed, 0.0)).astype(BF16)
        form1 = jnp.where(a > b, 2.0 * packed, jnp.where(a == b, diagonal, 0.0)).astype(BF16)
        for k in blocks:
            b0, b1 = three[0, pl.ds(k, step), :], three[1, pl.ds(k, step), :]
            product = jnp.dot(b0, form0, preferred_element_type=F32) * b0.astype(F32)
            product += jnp.dot(b1, form1, preferred_element_type=F32) * b1.astype(F32)
            emit(k, product[:, 0:LANES] + product[:, LANES:WID])


def ahead_kernel(step, own, three, ahead):
    def emit(k, partial):
        ahead[pl.ds(k, step), :] = partial

    quadratic(lax.axis_index("rep") == PACKED, own, three, step, emit)


def weight_kernel(window, per, step, starts, other, ahead, three, hot, padded, packs, sums, terms, tops, sem):
    rows = three.shape[1]
    copy = pltpu.make_async_copy(starts, tops, sem)
    copy.start()
    terms[...] = jnp.zeros(terms.shape, F32)

    def emit(k, partial):
        partial = partial + ahead[pl.ds(k, step), :]
        for q in range(0, step, LANES):
            weight = jnp.sum(partial[q : q + LANES].T, axis=0, keepdims=True)
            lanes = pl.ds(k + q, LANES)
            term = padded[:, lanes] * weight
            high = term.astype(BF16).astype(F32)
            stacked = jnp.concatenate([high, term - high], axis=0).astype(BF16)
            both = jnp.dot(stacked, hot[lanes, :], preferred_element_type=F32)
            sums[(k + q) // LANES] = both[0:8, :] + both[8:16, :]

    quadratic(lax.axis_index("rep") != PACKED, other, three, step, emit)
    copy.wait()
    for block in range(rows // LANES):
        value = sums[block]
        tile = tops[block, 0]
        for j in range(window):
            terms[tile + j] += value[:, j * LANES : (j + 1) * LANES]
    for owner in range(2 * packs.shape[0]):
        tile, lane = owner * per // LANES, owner * per % LANES
        value = terms[tile]
        if lane:
            value = pltpu.roll(value, LANES - lane, 1)
        if lane + per > LANES:
            value = jnp.where(iota(value.shape, 1) < LANES - lane, value, pltpu.roll(terms[tile + 1], LANES - lane, 1))
        packs[owner // 2, owner % 2 * 4 : owner % 2 * 4 + 4, :] = value[0:4, :]


def gamma_rows(table, three, begin, out):
    rows = pl.ds(begin, out.shape[1])
    both = jnp.concatenate([three[0, rows, :], three[1, rows, :]], axis=1)
    g = jnp.dot(both, table[...], preferred_element_type=F32)
    out[0] = g[:, 0:WID].astype(BF16)
    out[1] = g[:, WID:].astype(BF16)


def gamma_first(own, other, three, mine, kept, table, out):
    kept[...] = mine[...]
    part0, part1 = parts_of(own, other)
    a, b = iota((WID, WID), 0), iota((WID, WID), 1)
    t01 = part0[0:WID, :]
    packed = part1[0:WID, :]
    turned = packed.T.astype(F32)
    packed = packed.astype(F32)
    diagonal = part1[WID : WID + 1, :].astype(F32)
    table[0:WID, 0:WID] = jnp.where(a <= b, packed, turned).astype(BF16)
    table[0:WID, WID : 2 * WID] = t01
    table[WID : 2 * WID, 0:WID] = t01.T
    table[WID : 2 * WID, WID : 2 * WID] = jnp.where(a > b, packed, jnp.where(a == b, diagonal, turned)).astype(BF16)
    gamma_rows(table, three, 0, out)


def gamma_second(table, three, done, mine, gamma, kept, out, sem):
    copy = pltpu.make_async_copy(done, gamma.at[:, pl.ds(0, done.shape[1]), :], sem)
    copy.start()
    kept[...] = mine[...]
    gamma_rows(table, three, done.shape[1], out)
    copy.wait()


def gamma_last(done, mine, before, gamma, kept, sem):
    copy = pltpu.make_async_copy(done, gamma.at[:, pl.ds(done.shape[1], done.shape[1]), :], sem)
    copy.start()
    kept[...] = mine[...]
    copy.wait()


def swap(x, axis, bit):
    count = lax.axis_size(axis)
    return lax.ppermute(x, axis, [(i, i ^ bit) for i in range(count)])


def shards(
    three_index,
    valid_columns,
    domain_blocks,
    occupied_energy,
    virtual_energy,
    shell_index,
    centre_weights,
    *,
    shells,
):
    rows = three_index.shape[1]
    n_occ, n_aux, n_rep = lax.axis_size("occ"), lax.axis_size("aux"), lax.axis_size("rep")
    owners = n_occ * n_aux * n_rep
    per = shells // owners
    window = (LANES + SEG - 2) // LANES + 1
    tiles = -(-shells // LANES) + window
    vmem = pl.BlockSpec(memory_space=pltpu.VMEM)
    smem = pl.BlockSpec(memory_space=pltpu.SMEM)
    hbm = pl.BlockSpec(memory_space=pltpu.HBM)
    anywhere = pl.BlockSpec(memory_space=pl.ANY)

    def grant(mib):
        return pltpu.CompilerParams(vmem_limit_bytes=mib << 20)

    def cost(flops, size):
        return pl.CostEstimate(flops=flops, bytes_accessed=size, transcendentals=0)

    send, held = pl.pallas_call(
        functools.partial(send_kernel, PIECES),
        out_shape=(jax.ShapeDtypeStruct((PACK, WID), BF16), jax.ShapeDtypeStruct(three_index.shape, BF16)),
        in_specs=[hbm],
        out_specs=(vmem, vmem),
        scratch_shapes=[pltpu.SemaphoreType.DMA((len(PIECES),))],
        compiler_params=grant(51),
        cost_estimate=cost(4 * WID * WID * rows, 4 * WID * rows),
        name="send",
    )(three_index)
    keep = pl.pallas_call(
        keep_kernel,
        out_shape=jax.ShapeDtypeStruct((PACK, WID), F32),
        in_specs=[vmem],
        out_specs=vmem,
        compiler_params=grant(16),
        cost_estimate=cost(4 * WID * WID * rows, 4 * WID * rows),
        name="keep",
    )(held)
    factor, hot, padded, starts = pl.pallas_call(
        functools.partial(prep_kernel, window),
        out_shape=(
            jax.ShapeDtypeStruct((PACK, WID), F32),
            jax.ShapeDtypeStruct((rows, window * LANES), BF16),
            jax.ShapeDtypeStruct((8, rows), F32),
            jax.ShapeDtypeStruct((16, LANES), jnp.int32),
        ),
        in_specs=[smem, smem, smem, vmem, smem, vmem, vmem],
        out_specs=(vmem,) * 4,
        compiler_params=grant(16),
        cost_estimate=cost(4 * rows * window * LANES, 2 * rows * window * LANES),
        name="prep",
    )(
        valid_columns,
        domain_blocks,
        occupied_energy,
        virtual_energy.reshape(-1, VBW),
        shell_index,
        shell_index.reshape(-1, LANES),
        centre_weights,
    )

    sums = keep + swap(send, "rep", 1).astype(F32)
    bit = 1
    while bit < n_aux:
        sums = sums + swap(sums.astype(BF16), "aux", bit).astype(F32)
        bit *= 2
    own = (sums * factor).astype(BF16)
    other = swap(own, "rep", 1)

    step = rows
    ahead = pl.pallas_call(
        functools.partial(ahead_kernel, step),
        out_shape=jax.ShapeDtypeStruct((rows, LANES), F32),
        in_specs=[vmem] * 2,
        out_specs=vmem,
        compiler_params=grant(16),
        cost_estimate=cost(4 * WID * WID * rows, 4 * WID * rows),
        name="ahead",
    )(own, held)
    part = pl.pallas_call(
        functools.partial(weight_kernel, window, per, step),
        out_shape=jax.ShapeDtypeStruct((owners // 2, 8, LANES), F32),
        in_specs=[vmem] * 6,
        out_specs=vmem,
        scratch_shapes=[
            pltpu.VMEM((rows // LANES, 8, window * LANES), F32),
            pltpu.VMEM((tiles, 8, LANES), F32),
            pltpu.SMEM((16, LANES), jnp.int32),
            pltpu.SemaphoreType.DMA,
        ],
        compiler_params=grant(16),
        cost_estimate=cost(4 * WID * WID * rows, 4 * WID * rows),
        name="weight",
    )(starts, other, ahead, held, hot, padded)

    halves = jax.ShapeDtypeStruct((2, rows // 2, WID), BF16)
    whole = jax.ShapeDtypeStruct(three_index.shape, BF16)

    def like(x):
        return jax.ShapeDtypeStruct(x.shape, x.dtype)

    def block(x, index, count=1):
        return lax.dynamic_slice_in_dim(x, index * count, count, 0)

    place, core = lax.axis_index("occ"), lax.axis_index("rep")
    part = part.reshape(n_occ, n_aux, 8, LANES)
    bit = n_occ // 2
    while bit > 2:
        half = part.shape[0] // 2
        up = (place // bit) % 2
        part = block(part, up, half) + swap(block(part, 1 - up, half), "occ", bit)
        bit //= 2

    low = place % 4
    first = core == 0
    far, near = jnp.where(first, low ^ 1, low ^ 2), jnp.where(first, low, low ^ 3)
    its_far, its_near = jnp.where(first, low ^ 2, low ^ 1), jnp.where(first, low ^ 3, low)
    mine = jnp.concatenate([block(part, far), block(part, near)], axis=0)
    mine, table, done = pl.pallas_call(
        gamma_first,
        out_shape=(like(mine), jax.ShapeDtypeStruct((2 * WID, 2 * WID), BF16), halves),
        in_specs=[vmem] * 4,
        out_specs=(vmem,) * 3,
        compiler_params=grant(12),
        cost_estimate=cost(4 * WID * WID * rows, 4 * WID * rows),
        name="gamma_first",
    )(own, other, held, mine)
    mine_sums = mine + swap(jnp.concatenate([block(part, its_far), block(part, its_near)], axis=0), "rep", 1)
    pairs = [(i, r) for i in range(n_occ) for r in range(2)]
    across = [(2 * i + r, 2 * (i ^ (2 if r else 1)) + r) for i, r in pairs]
    beside = [(2 * i + r, 2 * (i ^ (3 if r else 1)) + r) for i, r in pairs]
    received = lax.ppermute(mine_sums[0], ("occ", "rep"), across)
    received1 = lax.ppermute(mine_sums[1], ("occ", "rep"), beside)
    gamma, kept, done = pl.pallas_call(
        gamma_second,
        out_shape=(whole, like(mine_sums[1]), halves),
        in_specs=[vmem] * 4,
        out_specs=(hbm, vmem, vmem),
        scratch_shapes=[pltpu.SemaphoreType.DMA],
        compiler_params=grant(12),
        cost_estimate=cost(4 * WID * WID * rows, 4 * WID * rows),
        name="gamma_second",
    )(table, held, done, mine_sums[1])
    part = received + jnp.where(first, kept, received1)

    bit = n_aux // 2
    while bit:
        half = part.shape[0] // 2
        up = (lax.axis_index("aux") // bit) % 2
        mine = block(part, up, half)
        if done is not None:
            gamma, mine = pl.pallas_call(
                gamma_last,
                out_shape=(whole, like(mine)),
                in_specs=[vmem, vmem, hbm],
                out_specs=(hbm, vmem),
                input_output_aliases={2: 0},
                scratch_shapes=[pltpu.SemaphoreType.DMA],
                compiler_params=grant(4),
                cost_estimate=cost(4 * WID * WID * rows, 4 * WID * rows),
                name="gamma_last",
            )(done, mine, gamma)
            done = None
        part = mine + swap(block(part, 1 - up, half), "aux", bit)
        bit //= 2
    part = part[0] + swap(part, "rep", 1)[0]
    shell_gradient = lax.dynamic_slice(part, (4 * core, 0), (3, per))
    return gamma, shell_gradient


def solution(mesh):

    def whole(three_index, valid_columns, domain_blocks, occupied_energy, virtual_energy, shell_index, centre_weights):
        shells = three_index.shape[1] // 5
        return jax.shard_map(
            functools.partial(shards, shells=shells),
            mesh=mesh,
            in_specs=(
                P(("pose", "occ"), ("aux", "rep"), None),
                P(("pose", "occ")),
                P(("pose", "occ"), None),
                P(("pose", "occ")),
                P("pose"),
                P(("aux", "rep")),
                P(None, ("pose", "aux", "rep")),
            ),
            out_specs=(
                P(("pose", "occ"), ("aux", "rep"), None),
                P(None, ("pose", "occ", "aux", "rep")),
            ),
            check_vma=False,
        )(three_index, valid_columns, domain_blocks, occupied_energy, virtual_energy, shell_index, centre_weights)

    return whole
```

```python
import functools
import jax
import jax.numpy as jnp
from jax import lax
from jax.experimental import pallas as pl
from jax.experimental.pallas import tpu as pltpu
from jax.sharding import PartitionSpec as P

VBW = 128
DOM = 2
WID = VBW * DOM
PACK = WID + 16
LANES = 128
SEG = 128
PACKED = 0
PIECES = (1280, 640)
OPPOSITE_SCALE = 1.3
F32 = jnp.float32
BF16 = jnp.bfloat16


def iota(shape, dim):
    return lax.broadcasted_iota(jnp.int32, shape, dim)


def slices(sizes):
    return [pl.ds(sum(sizes[:k]), size) for k, size in enumerate(sizes)]


def tdot(x, y):
    return lax.dot_general(x, y, (((0,), (0,)), ((), ())), preferred_element_type=F32)


def make_factor(valid, blocks, occupied, energies, factor):
    second = lax.axis_index("rep") == PACKED
    virtual = [
        jnp.concatenate([energies[pl.ds(blocks[i, d], 1), :] for d in range(DOM)], axis=1) for i in range(2)
    ]
    columns = jnp.concatenate([jnp.broadcast_to(v, (8, WID)) for v in virtual], axis=0).T
    down = [columns[:, 0:1], columns[:, 8:9]]
    a, b = iota((WID, WID), 0), iota((WID, WID), 1)
    upper = a <= b
    e0, e1 = occupied[0], occupied[1]
    v0, v1 = valid[0], valid[1]

    @pl.when(jnp.logical_not(second))
    def _():
        denominator = down[0] + virtual[1] - e0 - e1
        inside = (a < v0) & (b < v1)
        factor[0:WID, :] = jnp.where(inside, OPPOSITE_SCALE / denominator, 0.0)
        factor[WID:PACK, :] = jnp.zeros((PACK - WID, WID), F32)

    @pl.when(second)
    def _():
        denominator = jnp.where(upper, down[0] + virtual[0] - e0 - e0, down[1] + virtual[1] - e1 - e1)
        limit = jnp.where(upper, v0, v1)
        inside = (a < limit) & (b < limit)
        factor[0:WID, :] = jnp.where(inside, OPPOSITE_SCALE / denominator, 0.0)
        diagonal = jnp.broadcast_to(virtual[1] + virtual[1] - e1 - e1, (PACK - WID, WID))
        inside = iota((PACK - WID, WID), 1) < v1
        factor[WID:PACK, :] = jnp.where(inside, OPPOSITE_SCALE / diagonal, 0.0)


def gram_part(second, pieces, held, out, ready=lambda k: None):
    def total(pairs):
        sums = None
        for k, rows in enumerate(slices(pieces)):
            ready(k)
            terms = [tdot(held[i, rows, :], held[j, rows, :]) for i, j in pairs]
            sums = terms if sums is None else [x + y for x, y in zip(sums, terms)]
        return sums

    @pl.when(jnp.logical_not(second))
    def _():
        (c01,) = total([(0, 1)])
        out[0:WID, :] = c01.astype(out.dtype)
        out[WID:PACK, :] = jnp.zeros((PACK - WID, WID), out.dtype)

    @pl.when(second)
    def _():
        a, b = iota((WID, WID), 0), iota((WID, WID), 1)
        c00, c11 = total([(0, 0), (1, 1)])
        diagonal = jnp.sum(jnp.where(a == b, c11, 0.0), axis=0, keepdims=True)
        out[0:WID, :] = jnp.where(a <= b, c00, c11).astype(out.dtype)
        out[WID:PACK, :] = jnp.broadcast_to(diagonal, (PACK - WID, WID)).astype(out.dtype)


def send_kernel(pieces, three, send, held, sems):
    copies = []
    for k, rows in enumerate(slices(pieces)):
        copies.append(pltpu.make_async_copy(three.at[:, rows, :], held.at[:, rows, :], sems.at[k]))
        copies[-1].start()
    gram_part(lax.axis_index("rep") != PACKED, pieces, held, send, lambda k: copies[k].wait())


def keep_kernel(held, keep):
    gram_part(lax.axis_index("rep") == PACKED, [held.shape[1]], held, keep)


def prep_kernel(
    window, valid, blocks, occupied, energies, firsts, index, weights, factor, hot, padded, starts
):
    make_factor(valid, blocks, occupied, energies, factor)
    padded[...] = jnp.zeros(padded.shape, F32)
    padded[0:3, :] = weights[...]
    lanes = iota((LANES, LANES), 1)
    for k in range(index.shape[0]):
        block = k * LANES // SEG
        tile = lax.div(firsts[block * SEG], LANES)
        starts[block : block + 1, :] = jnp.full((1, LANES), tile, jnp.int32)
        column = index[k : k + 1, :] - tile * LANES
        turned = jnp.broadcast_to(column.astype(F32), (LANES, LANES)).T.astype(jnp.int32)
        for j in range(window):
            hot[pl.ds(k * LANES, LANES), pl.ds(j * LANES, LANES)] = (
                (turned == lanes + j * LANES).astype(F32).astype(BF16)
            )


def parts_of(own, other):
    first = lax.axis_index("rep") != PACKED
    return jnp.where(first, own[...], other[...]), jnp.where(first, other[...], own[...])


def sums_kernel(mine, received, sums, rounded):
    total = mine[...] + received[...].astype(F32)
    sums[...] = total
    rounded[...] = total.astype(BF16)


def quadratic(second, part, three, step, emit):
    blocks = range(0, three.shape[1], step)
    a, b = iota((WID, WID), 0), iota((WID, WID), 1)

    @pl.when(jnp.logical_not(second))
    def _():
        form = (2.0 * part[0:WID, :].astype(F32)).astype(BF16)
        for k in blocks:
            b0, b1 = three[0, pl.ds(k, step), :], three[1, pl.ds(k, step), :]
            product = jnp.dot(b0, form, preferred_element_type=F32) * b1.astype(F32)
            emit(k, product[:, 0:LANES] + product[:, LANES:WID])

    @pl.when(second)
    def _():
        packed = part[0:WID, :].astype(F32)
        diagonal = part[WID:PACK, :].astype(F32)[0:1, :]
        form0 = jnp.where(a < b, 2.0 * packed, jnp.where(a == b, packed, 0.0)).astype(BF16)
        form1 = jnp.where(a > b, 2.0 * packed, jnp.where(a == b, diagonal, 0.0)).astype(BF16)
        for k in blocks:
            b0, b1 = three[0, pl.ds(k, step), :], three[1, pl.ds(k, step), :]
            product = jnp.dot(b0, form0, preferred_element_type=F32) * b0.astype(F32)
            product += jnp.dot(b1, form1, preferred_element_type=F32) * b1.astype(F32)
            emit(k, product[:, 0:LANES] + product[:, LANES:WID])


def ahead_kernel(step, own, three, ahead):
    def emit(k, partial):
        ahead[pl.ds(k, step), :] = partial

    quadratic(lax.axis_index("rep") == PACKED, own, three, step, emit)


def weight_kernel(window, per, step, starts, other, ahead, three, hot, padded, packs, sums, terms):
    rows = three.shape[1]
    tops = [starts[block, 0] for block in range(rows // LANES)]
    terms[...] = jnp.zeros(terms.shape, F32)

    def emit(k, partial):
        partial = partial + ahead[pl.ds(k, step), :]
        for q in range(0, step, LANES):
            weight = jnp.sum(partial[q : q + LANES].T, axis=0, keepdims=True)
            lanes = pl.ds(k + q, LANES)
            term = padded[:, lanes] * weight
            high = term.astype(BF16).astype(F32)
            stacked = jnp.concatenate([high, term - high], axis=0).astype(BF16)
            both = jnp.dot(stacked, hot[lanes, :], preferred_element_type=F32)
            sums[(k + q) // LANES] = both[0:8, :] + both[8:16, :]

    quadratic(lax.axis_index("rep") != PACKED, other, three, step, emit)
    for block in range(rows // LANES):
        value = sums[block]
        tile = tops[block]
        for j in range(window):
            terms[tile + j] += value[:, j * LANES : (j + 1) * LANES]
    for owner in range(2 * packs.shape[0]):
        tile, lane = owner * per // LANES, owner * per % LANES
        value = terms[tile]
        if lane:
            value = pltpu.roll(value, LANES - lane, 1)
        if lane + per > LANES:
            value = jnp.where(iota(value.shape, 1) < LANES - lane, value, pltpu.roll(terms[tile + 1], LANES - lane, 1))
        packs[owner // 2, owner % 2 * 4 : owner % 2 * 4 + 4, :] = value[0:4, :]


def gamma_rows(table, three, begin, out):
    rows = pl.ds(begin, out.shape[1])
    both = jnp.concatenate([three[0, rows, :], three[1, rows, :]], axis=1)
    g = jnp.dot(both, table[...], preferred_element_type=F32)
    out[0] = g[:, 0:WID].astype(BF16)
    out[1] = g[:, WID:].astype(BF16)


def gamma_first(own, other, three, mine, kept, table, out):
    kept[...] = mine[...]
    part0, part1 = parts_of(own, other)
    a, b = iota((WID, WID), 0), iota((WID, WID), 1)
    t01 = part0[0:WID, :]
    packed = part1[0:WID, :]
    turned = packed.T.astype(F32)
    packed = packed.astype(F32)
    diagonal = part1[WID : WID + 1, :].astype(F32)
    table[0:WID, 0:WID] = jnp.where(a <= b, packed, turned).astype(BF16)
    table[0:WID, WID : 2 * WID] = t01
    table[WID : 2 * WID, 0:WID] = t01.T
    table[WID : 2 * WID, WID : 2 * WID] = jnp.where(a > b, packed, jnp.where(a == b, diagonal, turned)).astype(BF16)
    gamma_rows(table, three, 0, out)


def gamma_second(table, three, done, mine, gamma, kept, out, sems):
    size = done.shape[1]
    copies = [
        pltpu.make_async_copy(done, gamma.at[:, pl.ds(0, size), :], sems.at[0]),
        pltpu.make_async_copy(out, gamma.at[:, pl.ds(size, size), :], sems.at[1]),
    ]
    copies[0].start()
    kept[...] = mine[...]
    gamma_rows(table, three, size, out)
    copies[1].start()
    for copy in copies:
        copy.wait()


def swap(x, axis, bit):
    count = lax.axis_size(axis)
    return lax.ppermute(x, axis, [(i, i ^ bit) for i in range(count)])


def shards(
    three_index,
    valid_columns,
    domain_blocks,
    occupied_energy,
    virtual_energy,
    shell_index,
    centre_weights,
    *,
    shells,
):
    rows = three_index.shape[1]
    n_occ, n_aux, n_rep = lax.axis_size("occ"), lax.axis_size("aux"), lax.axis_size("rep")
    owners = n_occ * n_aux * n_rep
    per = shells // owners
    window = (LANES + SEG - 2) // LANES + 1
    tiles = -(-shells // LANES) + window
    vmem = pl.BlockSpec(memory_space=pltpu.VMEM)
    smem = pl.BlockSpec(memory_space=pltpu.SMEM)
    hbm = pl.BlockSpec(memory_space=pltpu.HBM)
    anywhere = pl.BlockSpec(memory_space=pl.ANY)

    def grant(mib):
        return pltpu.CompilerParams(vmem_limit_bytes=mib << 20)

    def cost(flops, size):
        return pl.CostEstimate(flops=flops, bytes_accessed=size, transcendentals=0)

    send, held = pl.pallas_call(
        functools.partial(send_kernel, PIECES),
        out_shape=(jax.ShapeDtypeStruct((PACK, WID), BF16), jax.ShapeDtypeStruct(three_index.shape, BF16)),
        in_specs=[hbm],
        out_specs=(vmem, vmem),
        scratch_shapes=[pltpu.SemaphoreType.DMA((len(PIECES),))],
        compiler_params=grant(51),
        cost_estimate=cost(4 * WID * WID * rows, 4 * WID * rows),
        name="send",
    )(three_index)
    keep = pl.pallas_call(
        keep_kernel,
        out_shape=jax.ShapeDtypeStruct((PACK, WID), F32),
        in_specs=[vmem],
        out_specs=vmem,
        compiler_params=grant(16),
        cost_estimate=cost(4 * WID * WID * rows, 4 * WID * rows),
        name="keep",
    )(held)
    factor, hot, padded, starts = pl.pallas_call(
        functools.partial(prep_kernel, window),
        out_shape=(
            jax.ShapeDtypeStruct((PACK, WID), F32),
            jax.ShapeDtypeStruct((rows, window * LANES), BF16),
            jax.ShapeDtypeStruct((8, rows), F32),
            jax.ShapeDtypeStruct((16, LANES), jnp.int32),
        ),
        in_specs=[smem, smem, smem, vmem, smem, vmem, vmem],
        out_specs=(vmem,) * 4,
        compiler_params=grant(16),
        cost_estimate=cost(4 * rows * window * LANES, 2 * rows * window * LANES),
        name="prep",
    )(
        valid_columns,
        domain_blocks,
        occupied_energy,
        virtual_energy.reshape(-1, VBW),
        shell_index,
        shell_index.reshape(-1, LANES),
        centre_weights,
    )

    sums, rounded = pl.pallas_call(
        sums_kernel,
        out_shape=(jax.ShapeDtypeStruct((PACK, WID), F32), jax.ShapeDtypeStruct((PACK, WID), BF16)),
        in_specs=[vmem] * 2,
        out_specs=(vmem, vmem),
        compiler_params=grant(4),
        name="sums",
    )(keep, swap(send, "rep", 1))
    bit = 1
    while bit < n_aux:
        sums = sums + swap(rounded, "aux", bit).astype(F32)
        rounded = sums.astype(BF16)
        bit *= 2
    own = (sums * factor).astype(BF16)
    other = swap(own, "rep", 1)

    step = rows
    ahead = pl.pallas_call(
        functools.partial(ahead_kernel, step),
        out_shape=jax.ShapeDtypeStruct((rows, LANES), F32),
        in_specs=[vmem] * 2,
        out_specs=vmem,
        compiler_params=grant(16),
        cost_estimate=cost(4 * WID * WID * rows, 4 * WID * rows),
        name="ahead",
    )(own, held)
    part = pl.pallas_call(
        functools.partial(weight_kernel, window, per, step),
        out_shape=jax.ShapeDtypeStruct((owners // 2, 8, LANES), F32),
        in_specs=[vmem] * 6,
        out_specs=vmem,
        scratch_shapes=[
            pltpu.VMEM((rows // LANES, 8, window * LANES), F32),
            pltpu.VMEM((tiles, 8, LANES), F32),
        ],
        compiler_params=grant(16),
        cost_estimate=cost(4 * WID * WID * rows, 4 * WID * rows),
        name="weight",
    )(starts, other, ahead, held, hot, padded)

    halves = jax.ShapeDtypeStruct((2, rows // 2, WID), BF16)
    whole = jax.ShapeDtypeStruct(three_index.shape, BF16)

    def like(x):
        return jax.ShapeDtypeStruct(x.shape, x.dtype)

    def block(x, index, count=1):
        return lax.dynamic_slice_in_dim(x, index * count, count, 0)

    place, core = lax.axis_index("occ"), lax.axis_index("rep")
    part = part.reshape(n_occ, n_aux, 8, LANES)
    bit = n_occ // 2
    while bit > 2:
        half = part.shape[0] // 2
        up = (place // bit) % 2
        part = block(part, up, half) + swap(block(part, 1 - up, half), "occ", bit)
        bit //= 2

    low = place % 4
    first = core == 0
    far, near = jnp.where(first, low ^ 1, low ^ 2), jnp.where(first, low, low ^ 3)
    its_far, its_near = jnp.where(first, low ^ 2, low ^ 1), jnp.where(first, low ^ 3, low)
    mine = jnp.concatenate([block(part, far), block(part, near)], axis=0)
    mine, table, done = pl.pallas_call(
        gamma_first,
        out_shape=(like(mine), jax.ShapeDtypeStruct((2 * WID, 2 * WID), BF16), halves),
        in_specs=[vmem] * 4,
        out_specs=(vmem,) * 3,
        compiler_params=grant(12),
        cost_estimate=cost(4 * WID * WID * rows, 4 * WID * rows),
        name="gamma_first",
    )(own, other, held, mine)
    mine_sums = mine + swap(jnp.concatenate([block(part, its_far), block(part, its_near)], axis=0), "rep", 1)
    pairs = [(i, r) for i in range(n_occ) for r in range(2)]
    across = [(2 * i + r, 2 * (i ^ (2 if r else 1)) + r) for i, r in pairs]
    beside = [(2 * i + r, 2 * (i ^ (3 if r else 1)) + r) for i, r in pairs]
    received = lax.ppermute(mine_sums[0], ("occ", "rep"), across)
    received1 = lax.ppermute(mine_sums[1], ("occ", "rep"), beside)
    gamma, kept = pl.pallas_call(
        gamma_second,
        out_shape=(whole, like(mine_sums[1])),
        in_specs=[vmem] * 4,
        out_specs=(hbm, vmem),
        scratch_shapes=[pltpu.VMEM(halves.shape, BF16), pltpu.SemaphoreType.DMA((2,))],
        compiler_params=grant(12),
        cost_estimate=cost(4 * WID * WID * rows, 4 * WID * rows),
        name="gamma_second",
    )(table, held, done, mine_sums[1])
    part = received + jnp.where(first, kept, received1)

    bit = n_aux // 2
    while bit:
        half = part.shape[0] // 2
        up = (lax.axis_index("aux") // bit) % 2
        mine = block(part, up, half)
        part = mine + swap(block(part, 1 - up, half), "aux", bit)
        bit //= 2
    part = part[0] + swap(part, "rep", 1)[0]
    shell_gradient = lax.dynamic_slice(part, (4 * core, 0), (3, per))
    return gamma, shell_gradient


def solution(mesh):

    def whole(three_index, valid_columns, domain_blocks, occupied_energy, virtual_energy, shell_index, centre_weights):
        shells = three_index.shape[1] // 5
        return jax.shard_map(
            functools.partial(shards, shells=shells),
            mesh=mesh,
            in_specs=(
                P(("pose", "occ"), ("aux", "rep"), None),
                P(("pose", "occ")),
                P(("pose", "occ"), None),
                P(("pose", "occ")),
                P("pose"),
                P(("aux", "rep")),
                P(None, ("pose", "aux", "rep")),
            ),
            out_specs=(
                P(("pose", "occ"), ("aux", "rep"), None),
                P(None, ("pose", "occ", "aux", "rep")),
            ),
            check_vma=False,
        )(three_index, valid_columns, domain_blocks, occupied_energy, virtual_energy, shell_index, centre_weights)

    return whole
```

```python
import functools
import jax
import jax.numpy as jnp
from jax import lax
from jax.experimental import pallas as pl
from jax.experimental.pallas import tpu as pltpu
from jax.sharding import PartitionSpec as P

VBW = 128
DOM = 2
WID = VBW * DOM
PACK = WID + 8
LANES = 128
SEG = 128
PACKED = 0
PIECES = (1280, 640)
OPPOSITE_SCALE = 1.3
F32 = jnp.float32
BF16 = jnp.bfloat16


def iota(shape, dim):
    return lax.broadcasted_iota(jnp.int32, shape, dim)


def slices(sizes):
    return [pl.ds(sum(sizes[:k]), size) for k, size in enumerate(sizes)]


def tdot(x, y):
    return lax.dot_general(x, y, (((0,), (0,)), ((), ())), preferred_element_type=F32)


def make_factor(valid, blocks, occupied, energies, factor):
    second = lax.axis_index("rep") == PACKED
    virtual = [
        jnp.concatenate([energies[pl.ds(blocks[i, d], 1), :] for d in range(DOM)], axis=1) for i in range(2)
    ]
    columns = jnp.concatenate([jnp.broadcast_to(v, (8, WID)) for v in virtual], axis=0).T
    down = [columns[:, 0:1], columns[:, 8:9]]
    a, b = iota((WID, WID), 0), iota((WID, WID), 1)
    upper = a <= b
    e0, e1 = occupied[0], occupied[1]
    v0, v1 = valid[0], valid[1]

    @pl.when(jnp.logical_not(second))
    def _():
        denominator = down[0] + virtual[1] - e0 - e1
        inside = (a < v0) & (b < v1)
        factor[0:WID, :] = jnp.where(inside, OPPOSITE_SCALE / denominator, 0.0)
        factor[WID:PACK, :] = jnp.zeros((PACK - WID, WID), F32)

    @pl.when(second)
    def _():
        denominator = jnp.where(upper, down[0] + virtual[0] - e0 - e0, down[1] + virtual[1] - e1 - e1)
        limit = jnp.where(upper, v0, v1)
        inside = (a < limit) & (b < limit)
        factor[0:WID, :] = jnp.where(inside, OPPOSITE_SCALE / denominator, 0.0)
        diagonal = jnp.broadcast_to(virtual[1] + virtual[1] - e1 - e1, (PACK - WID, WID))
        inside = iota((PACK - WID, WID), 1) < v1
        factor[WID:PACK, :] = jnp.where(inside, OPPOSITE_SCALE / diagonal, 0.0)


def gram_part(second, pieces, held, out, ready=lambda k: None):
    def total(pairs):
        sums = None
        for k, rows in enumerate(slices(pieces)):
            ready(k)
            terms = [tdot(held[i, rows, :], held[j, rows, :]) for i, j in pairs]
            sums = terms if sums is None else [x + y for x, y in zip(sums, terms)]
        return sums

    @pl.when(jnp.logical_not(second))
    def _():
        (c01,) = total([(0, 1)])
        out[0:WID, :] = c01.astype(out.dtype)
        out[WID:PACK, :] = jnp.zeros((PACK - WID, WID), out.dtype)

    @pl.when(second)
    def _():
        a, b = iota((WID, WID), 0), iota((WID, WID), 1)
        c00, c11 = total([(0, 0), (1, 1)])
        diagonal = jnp.sum(jnp.where(a == b, c11, 0.0), axis=0, keepdims=True)
        out[0:WID, :] = jnp.where(a <= b, c00, c11).astype(out.dtype)
        out[WID:PACK, :] = jnp.broadcast_to(diagonal, (PACK - WID, WID)).astype(out.dtype)


def send_kernel(pieces, three, send, held, sems):
    copies = []
    for k, rows in enumerate(slices(pieces)):
        copies.append(pltpu.make_async_copy(three.at[:, rows, :], held.at[:, rows, :], sems.at[k]))
        copies[-1].start()
    gram_part(lax.axis_index("rep") != PACKED, pieces, held, send, lambda k: copies[k].wait())


def keep_kernel(held, keep):
    gram_part(lax.axis_index("rep") == PACKED, [held.shape[1]], held, keep)


def prep_kernel(
    window, valid, blocks, occupied, energies, firsts, index, weights, factor, hot, padded, starts
):
    make_factor(valid, blocks, occupied, energies, factor)
    padded[...] = jnp.zeros(padded.shape, F32)
    padded[0:3, :] = weights[...]
    lanes = iota((LANES, LANES), 1)
    for k in range(index.shape[0]):
        block = k * LANES // SEG
        tile = lax.div(firsts[block * SEG], LANES)
        starts[block : block + 1, :] = jnp.full((1, LANES), tile, jnp.int32)
        column = index[k : k + 1, :] - tile * LANES
        turned = jnp.broadcast_to(column.astype(F32), (LANES, LANES)).T.astype(jnp.int32)
        for j in range(window):
            hot[pl.ds(k * LANES, LANES), pl.ds(j * LANES, LANES)] = (
                (turned == lanes + j * LANES).astype(F32).astype(BF16)
            )


def parts_of(own, other):
    first = lax.axis_index("rep") != PACKED
    return jnp.where(first, own[...], other[...]), jnp.where(first, other[...], own[...])


def sums_kernel(mine, received, sums, rounded):
    total = mine[...] + received[...].astype(F32)
    sums[...] = total
    rounded[...] = total.astype(BF16)


def quadratic(second, part, three, step, emit):
    blocks = range(0, three.shape[1], step)
    a, b = iota((WID, WID), 0), iota((WID, WID), 1)

    @pl.when(jnp.logical_not(second))
    def _():
        form = (2.0 * part[0:WID, :].astype(F32)).astype(BF16)
        for k in blocks:
            b0, b1 = three[0, pl.ds(k, step), :], three[1, pl.ds(k, step), :]
            product = jnp.dot(b0, form, preferred_element_type=F32) * b1.astype(F32)
            emit(k, product[:, 0:LANES] + product[:, LANES:WID])

    @pl.when(second)
    def _():
        packed = part[0:WID, :].astype(F32)
        diagonal = part[WID:PACK, :].astype(F32)[0:1, :]
        form0 = jnp.where(a < b, 2.0 * packed, jnp.where(a == b, packed, 0.0)).astype(BF16)
        form1 = jnp.where(a > b, 2.0 * packed, jnp.where(a == b, diagonal, 0.0)).astype(BF16)
        for k in blocks:
            b0, b1 = three[0, pl.ds(k, step), :], three[1, pl.ds(k, step), :]
            product = jnp.dot(b0, form0, preferred_element_type=F32) * b0.astype(F32)
            product += jnp.dot(b1, form1, preferred_element_type=F32) * b1.astype(F32)
            emit(k, product[:, 0:LANES] + product[:, LANES:WID])


def ahead_kernel(step, own, three, ahead):
    def emit(k, partial):
        ahead[pl.ds(k, step), :] = partial

    quadratic(lax.axis_index("rep") == PACKED, own, three, step, emit)


def weight_kernel(window, per, step, starts, other, ahead, three, hot, padded, packs, sums, terms):
    rows = three.shape[1]
    tops = [starts[block, 0] for block in range(rows // LANES)]
    terms[...] = jnp.zeros(terms.shape, F32)

    def emit(k, partial):
        partial = partial + ahead[pl.ds(k, step), :]
        for q in range(0, step, LANES):
            weight = jnp.sum(partial[q : q + LANES].T, axis=0, keepdims=True)
            lanes = pl.ds(k + q, LANES)
            term = padded[:, lanes] * weight
            high = term.astype(BF16).astype(F32)
            stacked = jnp.concatenate([high, term - high], axis=0).astype(BF16)
            both = jnp.dot(stacked, hot[lanes, :], preferred_element_type=F32)
            sums[(k + q) // LANES] = both[0:8, :] + both[8:16, :]

    quadratic(lax.axis_index("rep") != PACKED, other, three, step, emit)
    for block in range(rows // LANES):
        value = sums[block]
        tile = tops[block]
        for j in range(window):
            terms[tile + j] += value[:, j * LANES : (j + 1) * LANES]
    for owner in range(2 * packs.shape[0]):
        tile, lane = owner * per // LANES, owner * per % LANES
        value = terms[tile]
        if lane:
            value = pltpu.roll(value, LANES - lane, 1)
        if lane + per > LANES:
            value = jnp.where(iota(value.shape, 1) < LANES - lane, value, pltpu.roll(terms[tile + 1], LANES - lane, 1))
        packs[owner // 2, owner % 2 * 4 : owner % 2 * 4 + 4, :] = value[0:4, :]


def gamma_rows(table, three, begin, out):
    rows = pl.ds(begin, out.shape[1])
    both = jnp.concatenate([three[0, rows, :], three[1, rows, :]], axis=1)
    g = jnp.dot(both, table[...], preferred_element_type=F32)
    out[0] = g[:, 0:WID].astype(BF16)
    out[1] = g[:, WID:].astype(BF16)


def gamma_first(own, other, three, mine, kept, table, out):
    kept[...] = mine[...]
    part0, part1 = parts_of(own, other)
    a, b = iota((WID, WID), 0), iota((WID, WID), 1)
    t01 = part0[0:WID, :]
    packed = part1[0:WID, :]
    turned = packed.T.astype(F32)
    packed = packed.astype(F32)
    diagonal = part1[WID : WID + 1, :].astype(F32)
    table[0:WID, 0:WID] = jnp.where(a <= b, packed, turned).astype(BF16)
    table[0:WID, WID : 2 * WID] = t01
    table[WID : 2 * WID, 0:WID] = t01.T
    table[WID : 2 * WID, WID : 2 * WID] = jnp.where(a > b, packed, jnp.where(a == b, diagonal, turned)).astype(BF16)
    gamma_rows(table, three, 0, out)


def gamma_second(table, three, done, mine, gamma, kept, out, sems):
    size = done.shape[1]
    copies = [
        pltpu.make_async_copy(done, gamma.at[:, pl.ds(0, size), :], sems.at[0]),
        pltpu.make_async_copy(out, gamma.at[:, pl.ds(size, size), :], sems.at[1]),
    ]
    copies[0].start()
    kept[...] = mine[...]
    gamma_rows(table, three, size, out)
    copies[1].start()
    for copy in copies:
        copy.wait()


def swap(x, axis, bit):
    count = lax.axis_size(axis)
    return lax.ppermute(x, axis, [(i, i ^ bit) for i in range(count)])


def shards(
    three_index,
    valid_columns,
    domain_blocks,
    occupied_energy,
    virtual_energy,
    shell_index,
    centre_weights,
    *,
    shells,
):
    rows = three_index.shape[1]
    n_occ, n_aux, n_rep = lax.axis_size("occ"), lax.axis_size("aux"), lax.axis_size("rep")
    owners = n_occ * n_aux * n_rep
    per = shells // owners
    window = (LANES + SEG - 2) // LANES + 1
    tiles = -(-shells // LANES) + window
    vmem = pl.BlockSpec(memory_space=pltpu.VMEM)
    smem = pl.BlockSpec(memory_space=pltpu.SMEM)
    hbm = pl.BlockSpec(memory_space=pltpu.HBM)
    anywhere = pl.BlockSpec(memory_space=pl.ANY)

    def grant(mib):
        return pltpu.CompilerParams(vmem_limit_bytes=mib << 20)

    def cost(flops, size):
        return pl.CostEstimate(flops=flops, bytes_accessed=size, transcendentals=0)

    send, held = pl.pallas_call(
        functools.partial(send_kernel, PIECES),
        out_shape=(jax.ShapeDtypeStruct((PACK, WID), BF16), jax.ShapeDtypeStruct(three_index.shape, BF16)),
        in_specs=[hbm],
        out_specs=(vmem, vmem),
        scratch_shapes=[pltpu.SemaphoreType.DMA((len(PIECES),))],
        compiler_params=grant(51),
        cost_estimate=cost(4 * WID * WID * rows, 4 * WID * rows),
        name="send",
    )(three_index)
    keep = pl.pallas_call(
        keep_kernel,
        out_shape=jax.ShapeDtypeStruct((PACK, WID), F32),
        in_specs=[vmem],
        out_specs=vmem,
        compiler_params=grant(16),
        cost_estimate=cost(4 * WID * WID * rows, 4 * WID * rows),
        name="keep",
    )(held)
    factor, hot, padded, starts = pl.pallas_call(
        functools.partial(prep_kernel, window),
        out_shape=(
            jax.ShapeDtypeStruct((PACK, WID), F32),
            jax.ShapeDtypeStruct((rows, window * LANES), BF16),
            jax.ShapeDtypeStruct((8, rows), F32),
            jax.ShapeDtypeStruct((16, LANES), jnp.int32),
        ),
        in_specs=[smem, smem, smem, vmem, smem, vmem, vmem],
        out_specs=(vmem,) * 4,
        compiler_params=grant(16),
        cost_estimate=cost(4 * rows * window * LANES, 2 * rows * window * LANES),
        name="prep",
    )(
        valid_columns,
        domain_blocks,
        occupied_energy,
        virtual_energy.reshape(-1, VBW),
        shell_index,
        shell_index.reshape(-1, LANES),
        centre_weights,
    )

    sums, rounded = pl.pallas_call(
        sums_kernel,
        out_shape=(jax.ShapeDtypeStruct((PACK, WID), F32), jax.ShapeDtypeStruct((PACK, WID), BF16)),
        in_specs=[vmem] * 2,
        out_specs=(vmem, vmem),
        compiler_params=grant(4),
        name="sums",
    )(keep, swap(send, "rep", 1))
    bit = 1
    while bit < n_aux:
        sums = sums + swap(rounded, "aux", bit).astype(F32)
        rounded = sums.astype(BF16)
        bit *= 2
    own = (sums * factor).astype(BF16)
    other = swap(own, "rep", 1)

    step = rows
    ahead = pl.pallas_call(
        functools.partial(ahead_kernel, step),
        out_shape=jax.ShapeDtypeStruct((rows, LANES), F32),
        in_specs=[vmem] * 2,
        out_specs=vmem,
        compiler_params=grant(16),
        cost_estimate=cost(4 * WID * WID * rows, 4 * WID * rows),
        name="ahead",
    )(own, held)
    part = pl.pallas_call(
        functools.partial(weight_kernel, window, per, step),
        out_shape=jax.ShapeDtypeStruct((owners // 2, 8, LANES), F32),
        in_specs=[vmem] * 6,
        out_specs=vmem,
        scratch_shapes=[
            pltpu.VMEM((rows // LANES, 8, window * LANES), F32),
            pltpu.VMEM((tiles, 8, LANES), F32),
        ],
        compiler_params=grant(16),
        cost_estimate=cost(4 * WID * WID * rows, 4 * WID * rows),
        name="weight",
    )(starts, other, ahead, held, hot, padded)

    halves = jax.ShapeDtypeStruct((2, rows // 2, WID), BF16)
    whole = jax.ShapeDtypeStruct(three_index.shape, BF16)

    def like(x):
        return jax.ShapeDtypeStruct(x.shape, x.dtype)

    def block(x, index, count=1):
        return lax.dynamic_slice_in_dim(x, index * count, count, 0)

    place, core = lax.axis_index("occ"), lax.axis_index("rep")
    part = part.reshape(n_occ, n_aux, 8, LANES)
    bit = n_occ // 2
    while bit > 2:
        half = part.shape[0] // 2
        up = (place // bit) % 2
        part = block(part, up, half) + swap(block(part, 1 - up, half), "occ", bit)
        bit //= 2

    low = place % 4
    first = core == 0
    far, near = jnp.where(first, low ^ 1, low ^ 2), jnp.where(first, low, low ^ 3)
    its_far, its_near = jnp.where(first, low ^ 2, low ^ 1), jnp.where(first, low ^ 3, low)
    mine = jnp.concatenate([block(part, far), block(part, near)], axis=0)
    mine, table, done = pl.pallas_call(
        gamma_first,
        out_shape=(like(mine), jax.ShapeDtypeStruct((2 * WID, 2 * WID), BF16), halves),
        in_specs=[vmem] * 4,
        out_specs=(vmem,) * 3,
        compiler_params=grant(12),
        cost_estimate=cost(4 * WID * WID * rows, 4 * WID * rows),
        name="gamma_first",
    )(own, other, held, mine)
    mine_sums = mine + swap(jnp.concatenate([block(part, its_far), block(part, its_near)], axis=0), "rep", 1)
    pairs = [(i, r) for i in range(n_occ) for r in range(2)]
    across = [(2 * i + r, 2 * (i ^ (2 if r else 1)) + r) for i, r in pairs]
    beside = [(2 * i + r, 2 * (i ^ (3 if r else 1)) + r) for i, r in pairs]
    received = lax.ppermute(mine_sums[0], ("occ", "rep"), across)
    received1 = lax.ppermute(mine_sums[1], ("occ", "rep"), beside)
    gamma, kept = pl.pallas_call(
        gamma_second,
        out_shape=(whole, like(mine_sums[1])),
        in_specs=[vmem] * 4,
        out_specs=(hbm, vmem),
        scratch_shapes=[pltpu.VMEM(halves.shape, BF16), pltpu.SemaphoreType.DMA((2,))],
        compiler_params=grant(12),
        cost_estimate=cost(4 * WID * WID * rows, 4 * WID * rows),
        name="gamma_second",
    )(table, held, done, mine_sums[1])
    part = received + jnp.where(first, kept, received1)

    bit = n_aux // 2
    while bit:
        half = part.shape[0] // 2
        up = (lax.axis_index("aux") // bit) % 2
        mine = block(part, up, half)
        part = mine + swap(block(part, 1 - up, half), "aux", bit)
        bit //= 2
    part = part[0] + swap(part, "rep", 1)[0]
    shell_gradient = lax.dynamic_slice(part, (4 * core, 0), (3, per))
    return gamma, shell_gradient


def solution(mesh):

    def whole(three_index, valid_columns, domain_blocks, occupied_energy, virtual_energy, shell_index, centre_weights):
        shells = three_index.shape[1] // 5
        return jax.shard_map(
            functools.partial(shards, shells=shells),
            mesh=mesh,
            in_specs=(
                P(("pose", "occ"), ("aux", "rep"), None),
                P(("pose", "occ")),
                P(("pose", "occ"), None),
                P(("pose", "occ")),
                P("pose"),
                P(("aux", "rep")),
                P(None, ("pose", "aux", "rep")),
            ),
            out_specs=(
                P(("pose", "occ"), ("aux", "rep"), None),
                P(None, ("pose", "occ", "aux", "rep")),
            ),
            check_vma=False,
        )(three_index, valid_columns, domain_blocks, occupied_energy, virtual_energy, shell_index, centre_weights)

    return whole
```

```python
import functools
import jax
import jax.numpy as jnp
from jax import lax
from jax.experimental import pallas as pl
from jax.experimental.pallas import tpu as pltpu
from jax.sharding import PartitionSpec as P

VBW = 128
DOM = 2
WID = VBW * DOM
PACK = WID + 8
LANES = 128
SEG = 128
PACKED = 0
PIECES = (960, 960)
OPPOSITE_SCALE = 1.3
F32 = jnp.float32
BF16 = jnp.bfloat16


def iota(shape, dim):
    return lax.broadcasted_iota(jnp.int32, shape, dim)


def slices(sizes):
    return [pl.ds(sum(sizes[:k]), size) for k, size in enumerate(sizes)]


def tdot(x, y):
    return lax.dot_general(x, y, (((0,), (0,)), ((), ())), preferred_element_type=F32)


def make_factor(valid, blocks, occupied, energies, factor):
    second = lax.axis_index("rep") == PACKED
    virtual = [
        jnp.concatenate([energies[pl.ds(blocks[i, d], 1), :] for d in range(DOM)], axis=1) for i in range(2)
    ]
    columns = jnp.concatenate([jnp.broadcast_to(v, (8, WID)) for v in virtual], axis=0).T
    down = [columns[:, 0:1], columns[:, 8:9]]
    a, b = iota((WID, WID), 0), iota((WID, WID), 1)
    upper = a <= b
    e0, e1 = occupied[0], occupied[1]
    v0, v1 = valid[0], valid[1]

    @pl.when(jnp.logical_not(second))
    def _():
        denominator = down[0] + virtual[1] - e0 - e1
        inside = (a < v0) & (b < v1)
        factor[0:WID, :] = jnp.where(inside, OPPOSITE_SCALE / denominator, 0.0)
        factor[WID:PACK, :] = jnp.zeros((PACK - WID, WID), F32)

    @pl.when(second)
    def _():
        denominator = jnp.where(upper, down[0] + virtual[0] - e0 - e0, down[1] + virtual[1] - e1 - e1)
        limit = jnp.where(upper, v0, v1)
        inside = (a < limit) & (b < limit)
        factor[0:WID, :] = jnp.where(inside, OPPOSITE_SCALE / denominator, 0.0)
        diagonal = jnp.broadcast_to(virtual[1] + virtual[1] - e1 - e1, (PACK - WID, WID))
        inside = iota((PACK - WID, WID), 1) < v1
        factor[WID:PACK, :] = jnp.where(inside, OPPOSITE_SCALE / diagonal, 0.0)


def gram_part(second, pieces, held, out, ready=lambda k: None):
    def total(pairs):
        sums = None
        for k, rows in enumerate(slices(pieces)):
            ready(k)
            terms = [tdot(held[i, rows, :], held[j, rows, :]) for i, j in pairs]
            sums = terms if sums is None else [x + y for x, y in zip(sums, terms)]
        return sums

    @pl.when(jnp.logical_not(second))
    def _():
        (c01,) = total([(0, 1)])
        out[0:WID, :] = c01.astype(out.dtype)
        out[WID:PACK, :] = jnp.zeros((PACK - WID, WID), out.dtype)

    @pl.when(second)
    def _():
        a, b = iota((WID, WID), 0), iota((WID, WID), 1)
        c00, c11 = total([(0, 0), (1, 1)])
        diagonal = jnp.sum(jnp.where(a == b, c11, 0.0), axis=0, keepdims=True)
        out[0:WID, :] = jnp.where(a <= b, c00, c11).astype(out.dtype)
        out[WID:PACK, :] = jnp.broadcast_to(diagonal, (PACK - WID, WID)).astype(out.dtype)


def send_kernel(pieces, three, send, held, sems):
    copies = []
    for k, rows in enumerate(slices(pieces)):
        copies.append(pltpu.make_async_copy(three.at[:, rows, :], held.at[:, rows, :], sems.at[k]))
        copies[-1].start()
    gram_part(lax.axis_index("rep") != PACKED, pieces, held, send, lambda k: copies[k].wait())


def keep_kernel(held, keep):
    gram_part(lax.axis_index("rep") == PACKED, [held.shape[1]], held, keep)


def prep_kernel(
    window, valid, blocks, occupied, energies, firsts, index, weights, factor, hot, padded, starts
):
    make_factor(valid, blocks, occupied, energies, factor)
    padded[...] = jnp.zeros(padded.shape, F32)
    padded[0:3, :] = weights[...]
    lanes = iota((LANES, LANES), 1)
    for k in range(index.shape[0]):
        block = k * LANES // SEG
        tile = lax.div(firsts[block * SEG], LANES)
        starts[block : block + 1, :] = jnp.full((1, LANES), tile, jnp.int32)
        column = index[k : k + 1, :] - tile * LANES
        turned = jnp.broadcast_to(column.astype(F32), (LANES, LANES)).T.astype(jnp.int32)
        for j in range(window):
            hot[pl.ds(k * LANES, LANES), pl.ds(j * LANES, LANES)] = (
                (turned == lanes + j * LANES).astype(F32).astype(BF16)
            )


def parts_of(own, other):
    first = lax.axis_index("rep") != PACKED
    return jnp.where(first, own[...], other[...]), jnp.where(first, other[...], own[...])


def sums_kernel(mine, received, sums, rounded):
    total = mine[...] + received[...].astype(F32)
    sums[...] = total
    rounded[...] = total.astype(BF16)


def quadratic(second, part, three, step, emit):
    blocks = range(0, three.shape[1], step)
    a, b = iota((WID, WID), 0), iota((WID, WID), 1)

    @pl.when(jnp.logical_not(second))
    def _():
        form = (2.0 * part[0:WID, :].astype(F32)).astype(BF16)
        for k in blocks:
            b0, b1 = three[0, pl.ds(k, step), :], three[1, pl.ds(k, step), :]
            product = jnp.dot(b0, form, preferred_element_type=F32) * b1.astype(F32)
            emit(k, product[:, 0:LANES] + product[:, LANES:WID])

    @pl.when(second)
    def _():
        packed = part[0:WID, :].astype(F32)
        diagonal = part[WID:PACK, :].astype(F32)[0:1, :]
        form0 = jnp.where(a < b, 2.0 * packed, jnp.where(a == b, packed, 0.0)).astype(BF16)
        form1 = jnp.where(a > b, 2.0 * packed, jnp.where(a == b, diagonal, 0.0)).astype(BF16)
        for k in blocks:
            b0, b1 = three[0, pl.ds(k, step), :], three[1, pl.ds(k, step), :]
            product = jnp.dot(b0, form0, preferred_element_type=F32) * b0.astype(F32)
            product += jnp.dot(b1, form1, preferred_element_type=F32) * b1.astype(F32)
            emit(k, product[:, 0:LANES] + product[:, LANES:WID])


def ahead_kernel(step, own, three, ahead):
    def emit(k, partial):
        ahead[pl.ds(k, step), :] = partial

    quadratic(lax.axis_index("rep") == PACKED, own, three, step, emit)


def weight_kernel(window, per, step, starts, other, ahead, three, hot, padded, packs, sums, terms):
    rows = three.shape[1]
    tops = [starts[block, 0] for block in range(rows // LANES)]
    terms[...] = jnp.zeros(terms.shape, F32)

    def emit(k, partial):
        partial = partial + ahead[pl.ds(k, step), :]
        for q in range(0, step, LANES):
            weight = jnp.sum(partial[q : q + LANES].T, axis=0, keepdims=True)
            lanes = pl.ds(k + q, LANES)
            term = padded[:, lanes] * weight
            high = term.astype(BF16).astype(F32)
            stacked = jnp.concatenate([high, term - high], axis=0).astype(BF16)
            both = jnp.dot(stacked, hot[lanes, :], preferred_element_type=F32)
            sums[(k + q) // LANES] = both[0:8, :] + both[8:16, :]

    quadratic(lax.axis_index("rep") != PACKED, other, three, step, emit)
    for block in range(rows // LANES):
        value = sums[block]
        tile = tops[block]
        for j in range(window):
            terms[tile + j] += value[:, j * LANES : (j + 1) * LANES]
    for owner in range(2 * packs.shape[0]):
        tile, lane = owner * per // LANES, owner * per % LANES
        value = terms[tile]
        if lane:
            value = pltpu.roll(value, LANES - lane, 1)
        if lane + per > LANES:
            value = jnp.where(iota(value.shape, 1) < LANES - lane, value, pltpu.roll(terms[tile + 1], LANES - lane, 1))
        packs[owner // 2, owner % 2 * 4 : owner % 2 * 4 + 4, :] = value[0:4, :]


def gamma_rows(table, three, begin, out):
    rows = pl.ds(begin, out.shape[1])
    both = jnp.concatenate([three[0, rows, :], three[1, rows, :]], axis=1)
    g = jnp.dot(both, table[...], preferred_element_type=F32)
    out[0] = g[:, 0:WID].astype(BF16)
    out[1] = g[:, WID:].astype(BF16)


def gamma_first(own, other, three, mine, kept, table, out):
    kept[...] = mine[...]
    part0, part1 = parts_of(own, other)
    a, b = iota((WID, WID), 0), iota((WID, WID), 1)
    t01 = part0[0:WID, :]
    packed = part1[0:WID, :]
    turned = packed.T.astype(F32)
    packed = packed.astype(F32)
    diagonal = part1[WID : WID + 1, :].astype(F32)
    table[0:WID, 0:WID] = jnp.where(a <= b, packed, turned).astype(BF16)
    table[0:WID, WID : 2 * WID] = t01
    table[WID : 2 * WID, 0:WID] = t01.T
    table[WID : 2 * WID, WID : 2 * WID] = jnp.where(a > b, packed, jnp.where(a == b, diagonal, turned)).astype(BF16)
    gamma_rows(table, three, 0, out)


def gamma_second(table, three, done, mine, gamma, kept, out, sems):
    size = done.shape[1]
    copies = [
        pltpu.make_async_copy(done, gamma.at[:, pl.ds(0, size), :], sems.at[0]),
        pltpu.make_async_copy(out, gamma.at[:, pl.ds(size, size), :], sems.at[1]),
    ]
    copies[0].start()
    kept[...] = mine[...]
    gamma_rows(table, three, size, out)
    copies[1].start()
    for copy in copies:
        copy.wait()


def swap(x, axis, bit):
    count = lax.axis_size(axis)
    return lax.ppermute(x, axis, [(i, i ^ bit) for i in range(count)])


def shards(
    three_index,
    valid_columns,
    domain_blocks,
    occupied_energy,
    virtual_energy,
    shell_index,
    centre_weights,
    *,
    shells,
):
    rows = three_index.shape[1]
    n_occ, n_aux, n_rep = lax.axis_size("occ"), lax.axis_size("aux"), lax.axis_size("rep")
    owners = n_occ * n_aux * n_rep
    per = shells // owners
    window = (LANES + SEG - 2) // LANES + 1
    tiles = -(-shells // LANES) + window
    vmem = pl.BlockSpec(memory_space=pltpu.VMEM)
    smem = pl.BlockSpec(memory_space=pltpu.SMEM)
    hbm = pl.BlockSpec(memory_space=pltpu.HBM)
    anywhere = pl.BlockSpec(memory_space=pl.ANY)

    def grant(mib):
        return pltpu.CompilerParams(vmem_limit_bytes=mib << 20)

    def cost(flops, size):
        return pl.CostEstimate(flops=flops, bytes_accessed=size, transcendentals=0)

    send, held = pl.pallas_call(
        functools.partial(send_kernel, PIECES),
        out_shape=(jax.ShapeDtypeStruct((PACK, WID), BF16), jax.ShapeDtypeStruct(three_index.shape, BF16)),
        in_specs=[hbm],
        out_specs=(vmem, vmem),
        scratch_shapes=[pltpu.SemaphoreType.DMA((len(PIECES),))],
        compiler_params=grant(51),
        cost_estimate=cost(4 * WID * WID * rows, 4 * WID * rows),
        name="send",
    )(three_index)
    keep = pl.pallas_call(
        keep_kernel,
        out_shape=jax.ShapeDtypeStruct((PACK, WID), F32),
        in_specs=[vmem],
        out_specs=vmem,
        compiler_params=grant(16),
        cost_estimate=cost(4 * WID * WID * rows, 4 * WID * rows),
        name="keep",
    )(held)
    factor, hot, padded, starts = pl.pallas_call(
        functools.partial(prep_kernel, window),
        out_shape=(
            jax.ShapeDtypeStruct((PACK, WID), F32),
            jax.ShapeDtypeStruct((rows, window * LANES), BF16),
            jax.ShapeDtypeStruct((8, rows), F32),
            jax.ShapeDtypeStruct((16, LANES), jnp.int32),
        ),
        in_specs=[smem, smem, smem, vmem, smem, vmem, vmem],
        out_specs=(vmem,) * 4,
        compiler_params=grant(16),
        cost_estimate=cost(4 * rows * window * LANES, 2 * rows * window * LANES),
        name="prep",
    )(
        valid_columns,
        domain_blocks,
        occupied_energy,
        virtual_energy.reshape(-1, VBW),
        shell_index,
        shell_index.reshape(-1, LANES),
        centre_weights,
    )

    sums, rounded = pl.pallas_call(
        sums_kernel,
        out_shape=(jax.ShapeDtypeStruct((PACK, WID), F32), jax.ShapeDtypeStruct((PACK, WID), BF16)),
        in_specs=[vmem] * 2,
        out_specs=(vmem, vmem),
        compiler_params=grant(4),
        name="sums",
    )(keep, swap(send, "rep", 1))
    bit = 1
    while bit < n_aux:
        sums = sums + swap(rounded, "aux", bit).astype(F32)
        rounded = sums.astype(BF16)
        bit *= 2
    own = (sums * factor).astype(BF16)
    other = swap(own, "rep", 1)

    step = rows
    ahead = pl.pallas_call(
        functools.partial(ahead_kernel, step),
        out_shape=jax.ShapeDtypeStruct((rows, LANES), F32),
        in_specs=[vmem] * 2,
        out_specs=vmem,
        compiler_params=grant(16),
        cost_estimate=cost(4 * WID * WID * rows, 4 * WID * rows),
        name="ahead",
    )(own, held)
    part = pl.pallas_call(
        functools.partial(weight_kernel, window, per, step),
        out_shape=jax.ShapeDtypeStruct((owners // 2, 8, LANES), F32),
        in_specs=[vmem] * 6,
        out_specs=vmem,
        scratch_shapes=[
            pltpu.VMEM((rows // LANES, 8, window * LANES), F32),
            pltpu.VMEM((tiles, 8, LANES), F32),
        ],
        compiler_params=grant(16),
        cost_estimate=cost(4 * WID * WID * rows, 4 * WID * rows),
        name="weight",
    )(starts, other, ahead, held, hot, padded)

    halves = jax.ShapeDtypeStruct((2, rows // 2, WID), BF16)
    whole = jax.ShapeDtypeStruct(three_index.shape, BF16)

    def like(x):
        return jax.ShapeDtypeStruct(x.shape, x.dtype)

    def block(x, index, count=1):
        return lax.dynamic_slice_in_dim(x, index * count, count, 0)

    place, core = lax.axis_index("occ"), lax.axis_index("rep")
    part = part.reshape(n_occ, n_aux, 8, LANES)
    bit = n_occ // 2
    while bit > 2:
        half = part.shape[0] // 2
        up = (place // bit) % 2
        part = block(part, up, half) + swap(block(part, 1 - up, half), "occ", bit)
        bit //= 2

    low = place % 4
    first = core == 0
    far, near = jnp.where(first, low ^ 1, low ^ 2), jnp.where(first, low, low ^ 3)
    its_far, its_near = jnp.where(first, low ^ 2, low ^ 1), jnp.where(first, low ^ 3, low)
    mine = jnp.concatenate([block(part, far), block(part, near)], axis=0)
    mine, table, done = pl.pallas_call(
        gamma_first,
        out_shape=(like(mine), jax.ShapeDtypeStruct((2 * WID, 2 * WID), BF16), halves),
        in_specs=[vmem] * 4,
        out_specs=(vmem,) * 3,
        compiler_params=grant(12),
        cost_estimate=cost(4 * WID * WID * rows, 4 * WID * rows),
        name="gamma_first",
    )(own, other, held, mine)
    mine_sums = mine + swap(jnp.concatenate([block(part, its_far), block(part, its_near)], axis=0), "rep", 1)
    pairs = [(i, r) for i in range(n_occ) for r in range(2)]
    across = [(2 * i + r, 2 * (i ^ (2 if r else 1)) + r) for i, r in pairs]
    beside = [(2 * i + r, 2 * (i ^ (3 if r else 1)) + r) for i, r in pairs]
    received = lax.ppermute(mine_sums[0], ("occ", "rep"), across)
    received1 = lax.ppermute(mine_sums[1], ("occ", "rep"), beside)
    gamma, kept = pl.pallas_call(
        gamma_second,
        out_shape=(whole, like(mine_sums[1])),
        in_specs=[vmem] * 4,
        out_specs=(hbm, vmem),
        scratch_shapes=[pltpu.VMEM(halves.shape, BF16), pltpu.SemaphoreType.DMA((2,))],
        compiler_params=grant(12),
        cost_estimate=cost(4 * WID * WID * rows, 4 * WID * rows),
        name="gamma_second",
    )(table, held, done, mine_sums[1])
    part = received + jnp.where(first, kept, received1)

    bit = n_aux // 2
    while bit:
        half = part.shape[0] // 2
        up = (lax.axis_index("aux") // bit) % 2
        mine = block(part, up, half)
        part = mine + swap(block(part, 1 - up, half), "aux", bit)
        bit //= 2
    part = part[0] + swap(part, "rep", 1)[0]
    shell_gradient = lax.dynamic_slice(part, (4 * core, 0), (3, per))
    return gamma, shell_gradient


def solution(mesh):

    def whole(three_index, valid_columns, domain_blocks, occupied_energy, virtual_energy, shell_index, centre_weights):
        shells = three_index.shape[1] // 5
        return jax.shard_map(
            functools.partial(shards, shells=shells),
            mesh=mesh,
            in_specs=(
                P(("pose", "occ"), ("aux", "rep"), None),
                P(("pose", "occ")),
                P(("pose", "occ"), None),
                P(("pose", "occ")),
                P("pose"),
                P(("aux", "rep")),
                P(None, ("pose", "aux", "rep")),
            ),
            out_specs=(
                P(("pose", "occ"), ("aux", "rep"), None),
                P(None, ("pose", "occ", "aux", "rep")),
            ),
            check_vma=False,
        )(three_index, valid_columns, domain_blocks, occupied_energy, virtual_energy, shell_index, centre_weights)

    return whole
```
